32 devices in a mesh: wide: 8 (over y, x, core), grp: 4 (over z).
Axes of the slice: x: 2, y: 2, z: 4, core: 2. Of those that a mesh axis runs over, the one named last changes fastest.
Arguments:
- embeds: bfloat16 [9216, 1024], P(('wide', 'grp')), may hold values from -700 to 700
- bucket: int32 [9216], P(('wide', 'grp')), may hold values from 0 to 7, as said below
- pairs: int32 [128], P(('wide', 'grp')), may hold values from -1 to 3, as said below
Outputs:
- density: float32 [32, 384], P(('wide', 'grp'))
The draws below stay inside these ranges and needn't reach their ends.
Inputs may be any that keep to these rules, and one draw needn't show every extreme that they name: At most 48 rows of one file shard name the same bucket; for every g some bucket is named by exactly 48 rows of every shard (s, g). `pairs`: the 4 entries of block (o, g) name distinct blocks (o, b) by b, live entries first and -1 after; for every o some block has all 4 entries live.
All inputs are finite; a program needn't handle non-finite values.
Results may differ from the reference program's by a relative error of at most 0.0034.
Values may be sent and summed in bfloat16 or wider, within the bound.
A program may use at most 64 MiB of HBM per device.

```python
import jax
import jax.numpy as jnp
from jax import lax

D = 1024
BLK = 384
ROW_DEV = 288
CAP = 48
PAIR_DEV = 4
ROWS = 9216
N_WIDE = 8
N_GRP = 4


def distinct_order(rand_key, dimensions):
    length = dimensions[-1]
    raw_bits = jax.random.randint(rand_key, dimensions, 0, 1 << 20)
    scores = raw_bits * length + jnp.arange(length, dtype=jnp.int32)
    return jnp.argsort(scores, axis=-1).astype(jnp.int32)


def draw_embeds(key, part):
    topic_key, pick_key, jitter_key = jax.random.split(key, 3)
    topics = jnp.clip(jax.random.normal(topic_key, (64, D), jnp.float32), -4.0, 4.0)
    chosen = jax.random.randint(pick_key, (ROWS,), 0, 64)
    jitter = jnp.clip(jax.random.normal(jitter_key, (ROWS, D), jnp.float32), -4.0, 4.0)
    values = topics[chosen] + 0.6 * jitter
    return values.astype(jnp.bfloat16)


def draw_bucket(key, part):
    full_key, count_key, order_key, shuffle_key = jax.random.split(key, 4)
    shards = N_WIDE * N_GRP
    others = N_WIDE - 1
    remaining = ROW_DEV - CAP
    lowest = max(1, -(-remaining // others))
    full_bucket = jax.random.randint(full_key, (N_GRP,), 0, N_WIDE)
    full_shard = jnp.tile(full_bucket, N_WIDE)
    amounts = jax.random.randint(count_key, (shards, others), lowest, CAP + 1)
    running_total = jnp.cumsum(amounts, axis=1)
    positions = jnp.arange(remaining, dtype=jnp.int32)
    picked = jnp.sum((running_total[:, None, :] <= positions[None, :, None]).astype(jnp.int32), axis=2)
    ordering = distinct_order(order_key, (shards, others))
    chosen = jnp.take_along_axis(ordering, picked, axis=1)
    other_bucket = (full_shard[:, None] + 1 + chosen) % N_WIDE
    sequence = jnp.concatenate([jnp.broadcast_to(full_shard[:, None], (shards, CAP)), other_bucket], axis=1)
    shuffle = distinct_order(shuffle_key, (shards, ROW_DEV))
    return jnp.take_along_axis(sequence, shuffle, axis=1).reshape(-1).astype(jnp.int32)


def draw_pairs(key, part):
    order_key, live_key, full_key = jax.random.split(key, 3)
    shards = N_WIDE * N_GRP
    ordering = distinct_order(order_key, (shards, N_GRP))[:, :PAIR_DEV]
    divisor = 1 + jax.random.randint(live_key, (shards,), 0, 2)
    live_count = PAIR_DEV // divisor
    full_member = jax.random.randint(full_key, (N_WIDE,), 0, N_GRP)
    member_index = jnp.arange(shards, dtype=jnp.int32) % N_GRP
    busiest = jnp.repeat(full_member, N_GRP) == member_index
    live_count = jnp.where(busiest, PAIR_DEV, live_count)
    slot_index = jnp.arange(PAIR_DEV, dtype=jnp.int32)
    entries = jnp.where(slot_index[None, :] < live_count[:, None], ordering, -1)
    return entries.reshape(-1).astype(jnp.int32)


def setup_inputs(seed: int = 0) -> dict:
    seeds = jax.random.split(jax.random.key(seed), 4)
    return {
        "embeds": draw_embeds(jax.random.fold_in(seeds[3], 71), 0),
        "bucket": draw_bucket(jax.random.fold_in(seeds[3], 71), 0),
        "pairs": draw_pairs(jax.random.fold_in(seeds[3], 71), 0),
    }


SHARPNESS = 10.0
EPSILON = 1e-06

def normalize(embeds):
    floats = embeds.astype(jnp.float32)
    return (floats * lax.rsqrt(lax.optimization_barrier(jnp.sum(floats * floats, axis=1, keepdims=True)) + EPSILON)).astype(jnp.bfloat16)

def reference(embeds, bucket, pairs):
    unit_rows = normalize(embeds).reshape(N_WIDE, N_GRP, ROW_DEV, D)
    owners = bucket.reshape(N_WIDE, N_GRP, ROW_DEV)
    onehot = (owners[..., None] == jnp.arange(N_WIDE, dtype=jnp.int32)).astype(jnp.int32)
    row_ranks = lax.optimization_barrier(jnp.sum(jnp.cumsum(onehot, axis=2) * onehot, axis=3)) - 1
    counts = lax.optimization_barrier(jnp.sum(onehot, axis=2))
    offsets = jnp.cumsum(counts, axis=0) - counts
    starts = jnp.take_along_axis(offsets, owners, axis=2)
    positions = (starts + row_ranks).astype(jnp.int32)
    totals = lax.optimization_barrier(jnp.sum(counts, axis=0)).T
    member = jnp.broadcast_to(jnp.arange(N_GRP, dtype=jnp.int32)[None, :, None], owners.shape)
    blocks = jnp.zeros((N_WIDE, N_GRP, BLK, D), jnp.bfloat16).at[owners, member, positions].set(unit_rows)
    valid_rows = (jnp.arange(BLK, dtype=jnp.int32)[None, None, :] < totals[:, :, None]).astype(jnp.float32)
    pair_lists = pairs.reshape(N_WIDE, N_GRP, PAIR_DEV)

    def one_owner(operands):
        owner_blocks, owner_flags, owner_lists = operands

        def one_shard(pieces):
            own_block, row_flags, entries = pieces
            live_count = jnp.sum((entries >= 0).astype(jnp.int32))
            left_rows = own_block.astype(jnp.float32)

            def add_pair(pair_index, running):
                target = entries[pair_index].astype(jnp.int32)
                right_rows = lax.dynamic_index_in_dim(owner_blocks, target, 0, keepdims=False).astype(jnp.float32)
                right_flags = lax.dynamic_index_in_dim(owner_flags, target, 0, keepdims=False)
                cosines = jnp.dot(left_rows, right_rows.T, precision=lax.Precision.HIGHEST)
                return running + lax.optimization_barrier(jnp.sum(jnp.exp(SHARPNESS * (cosines - 1.0)) * right_flags[None, :], axis=1))
            summed = lax.fori_loop(0, live_count, add_pair, jnp.zeros((BLK,), jnp.float32))
            return summed * row_flags
        return lax.map(one_shard, (owner_blocks, owner_flags, owner_lists))
    density = lax.map(one_owner, (blocks, valid_rows, pair_lists))
    return density.reshape(N_WIDE * N_GRP, BLK)
```

```python
import jax
import jax.numpy as jnp
from jax import lax
from jax.experimental import pallas as pl
from jax.experimental.pallas import tpu as pltpu
from jax.sharding import PartitionSpec as P
import functools
import math

BLK = 384


SHARPNESS = 10.0
EPSILON = 1e-06


def pair_sums(left_rows, right_rows, right_weight):
    cosines = lax.dot_general(
        left_rows, right_rows, (((1,), (1,)), ((), ())), preferred_element_type=jnp.float32
    )
    return jnp.sum(jnp.exp(SHARPNESS * (cosines - 1.0)) * right_weight[None, :], axis=1)


def per_device(embeds, bucket, pairs):
    wide_count = lax.axis_size("wide")
    feature_width = embeds.shape[1]
    capacity = BLK // wide_count
    floats = embeds.astype(jnp.float32)
    unit_rows = (
        floats * lax.rsqrt(jnp.sum(floats * floats, axis=1, keepdims=True) + EPSILON)
    ).astype(jnp.bfloat16)
    onehot = (bucket[:, None] == jnp.arange(wide_count, dtype=jnp.int32)[None, :]).astype(jnp.int32)
    row_ranks = jnp.sum(jnp.cumsum(onehot, axis=0) * onehot, axis=1) - 1
    counts = jnp.sum(onehot, axis=0)
    send_slots = bucket * capacity + row_ranks
    outgoing = (
        jnp.zeros((wide_count * capacity, feature_width), jnp.bfloat16)
        .at[send_slots]
        .set(unit_rows)
    )
    received, arrived = (
        lax.all_to_all(
            outgoing.reshape(wide_count, capacity, feature_width),
            "wide",
            split_axis=0,
            concat_axis=0,
            tiled=True,
        ),
        lax.all_to_all(
            counts.reshape(wide_count, 1), "wide", split_axis=0, concat_axis=0, tiled=True
        ),
    )
    arrived = arrived.reshape(wide_count)
    offsets = jnp.cumsum(arrived) - arrived
    within = jnp.arange(capacity, dtype=jnp.int32)
    places = jnp.where(within[None, :] < arrived[:, None], offsets[:, None] + within[None, :], BLK)
    own_block = (
        jnp.zeros((BLK, feature_width), jnp.bfloat16)
        .at[places.reshape(-1)]
        .set(received.reshape(wide_count * capacity, feature_width), mode="drop")
    )
    total_rows = jnp.sum(arrived)
    valid_rows = (jnp.arange(BLK, dtype=jnp.int32) < total_rows).astype(jnp.float32)
    flags_wire = valid_rows.astype(jnp.bfloat16)
    live_count = jnp.sum((pairs >= 0).astype(jnp.int32))
    first_row = jnp.int32(0)
    panel_rows = lax.all_gather(own_block, "grp", axis=0, tiled=True)
    panel_flags = lax.all_gather(flags_wire, "grp", axis=0, tiled=True)
    length = panel_rows.shape[0]
    span_rows = min(BLK, length)

    def add_pair(pair_index, running_sum):
        target = pairs[pair_index] * BLK
        shift_rows = jnp.clip(target, 0, length - span_rows)

        def add_tile(before):
            right_rows = lax.dynamic_slice_in_dim(panel_rows, shift_rows, span_rows, 0)
            right_flags = lax.dynamic_slice_in_dim(panel_flags, shift_rows, span_rows, 0).astype(
                jnp.float32
            )
            global_rows = shift_rows + jnp.arange(span_rows, dtype=jnp.int32)
            inside = (global_rows >= target) & (global_rows < target + BLK)
            return before + pair_sums(own_block, right_rows, jnp.where(inside, right_flags, 0.0))

        touches = (target < first_row + length) & (target + BLK > first_row)
        return lax.cond(touches, add_tile, lambda before: before, running_sum)

    density = lax.fori_loop(0, live_count, add_pair, jnp.zeros((BLK,), jnp.float32))
    return (density * valid_rows).reshape(1, BLK)


def general(mesh):
    placed = (P(("wide", "grp"), None), P(("wide", "grp")), P(("wide", "grp")))
    return jax.shard_map(
        per_device, mesh=mesh, in_specs=placed, out_specs=P(("wide", "grp"), None), check_vma=False
    )


MESH = pl.DeviceIdType.MESH
SCALE = SHARPNESS * math.log2(math.e)
NEVER = -1e30
MARK = 4.0
HALVES = 2


def rows_times_rows(left, right, precision=None):
    return lax.dot_general(
        left, right, (((1,), (1,)), ((), ())), precision=precision,
        preferred_element_type=jnp.float32,
    )


def gather_kernel(
    n_wide, n_grp, cap, embeds_ref, bucket_ref, pairs_ref, out_ref,
    rows, outgoing, panel, part, sums, result,
    load_sem, send_sem, recv_sem, give_sem, take_sem,
):
    me_wide, me_grp = lax.axis_index("wide"), lax.axis_index("grp")
    parity = lax.rem(me_wide, 2)
    my_home = n_grp // 2 - parity
    is_home = me_grp == my_home
    row_dev, width = rows.shape
    block = n_wide * cap
    devices = n_wide * n_grp

    def home_of(bucket_index):
        return n_grp // 2 - lax.rem(bucket_index, 2)

    def order_of(grp, odd):
        along = grp + odd * (n_grp - 1 - 2 * grp)
        return jnp.where(along >= n_grp // 2, along - n_grp // 2, n_grp - 1 - along)

    def grp_of(order, odd):
        along = order + n_grp // 2 if order < n_grp // 2 else n_grp - 1 - order
        return along + odd * (n_grp - 1 - 2 * along)

    load = pltpu.make_async_copy(embeds_ref, rows, load_sem)
    load.start()
    barrier = pltpu.get_barrier_semaphore()

    @pl.when(is_home)
    def _():
        def greet(step, carry):
            other = lax.rem(me_wide * n_grp + me_grp + step, devices)
            pl.semaphore_signal(
                barrier, inc=1, device_id=(other // n_grp, lax.rem(other, n_grp)),
                device_id_type=MESH,
            )
            return carry

        lax.fori_loop(1, devices, greet, 0)

    @pl.when(jnp.logical_not(is_home))
    def _():
        pl.semaphore_signal(
            barrier, inc=1, device_id=(me_wide, my_home), device_id_type=MESH
        )

    bucket = bucket_ref[...]
    of_bucket = lax.broadcasted_iota(jnp.int32, (n_wide, row_dev), 0) == bucket
    onehot = of_bucket.astype(jnp.float32)
    earlier = (
        lax.broadcasted_iota(jnp.int32, (row_dev, row_dev), 0)
        < lax.broadcasted_iota(jnp.int32, (row_dev, row_dev), 1)
    ).astype(jnp.float32).astype(jnp.bfloat16)
    before = jnp.dot(onehot.astype(jnp.bfloat16), earlier, preferred_element_type=jnp.float32)
    rank = jnp.sum(before * onehot, axis=0, keepdims=True).astype(jnp.int32)
    counts = jnp.sum(onehot, axis=1, keepdims=True).astype(jnp.int32)
    slots = bucket * cap + rank
    chosen = (
        lax.broadcasted_iota(jnp.int32, (block, row_dev), 0) == slots
    ).astype(jnp.float32).astype(jnp.bfloat16)

    load.wait()
    floats = rows[...].astype(jnp.float32)
    unit = (
        floats * lax.rsqrt(jnp.sum(floats * floats, axis=1, keepdims=True) + EPSILON)
    ).astype(jnp.bfloat16)
    placed = jnp.dot(chosen, unit, preferred_element_type=jnp.float32)
    first_lane = lax.broadcasted_iota(jnp.int32, (cap, 128), 1) == 0
    within = lax.broadcasted_iota(jnp.int32, (cap, 128), 0)
    for o in range(n_wide):
        piece = placed[o * cap : (o + 1) * cap]
        padding = first_lane & (within >= counts[o : o + 1, :])
        outgoing[o, :, :128] = jnp.where(padding, MARK, piece[:, :128]).astype(jnp.bfloat16)
        outgoing[o, :, 128:] = piece[:, 128:].astype(jnp.bfloat16)

    @pl.when(is_home)
    def _():
        pl.semaphore_wait(barrier, n_wide - 1 + n_grp - 1)

    @pl.when(jnp.logical_not(is_home))
    def _():
        pl.semaphore_wait(barrier, n_wide)

    def piece_copy(o):
        place = order_of(me_grp, lax.rem(o, 2)) * n_wide + me_wide
        return pltpu.make_async_remote_copy(
            src_ref=outgoing.at[o], dst_ref=panel.at[place],
            send_sem=send_sem.at[o], recv_sem=recv_sem.at[place],
            device_id=(o, home_of(o)), device_id_type=MESH,
        )

    for step in range(1, n_wide):
        piece_copy(lax.rem(me_wide + step, n_wide)).start()

    @pl.when(jnp.logical_not(is_home))
    def _():
        piece_copy(me_wide).start()

    @pl.when(is_home)
    def _():
        place = order_of(me_grp, parity) * n_wide + me_wide
        own = pltpu.make_async_copy(outgoing.at[me_wide], panel.at[place], recv_sem.at[place])
        own.start()
        unit_pieces = n_wide // HALVES
        unit_rows = block // HALVES
        lane_bias = []
        pick = (
            (lax.broadcasted_iota(jnp.int32, (8, 128), 1) == 0)
            .astype(jnp.float32).astype(jnp.bfloat16)
        )
        ones = jnp.ones((8, 128), jnp.float32)
        for k in range(n_grp):
            row_bias = []
            for h in range(HALVES):
                first = k * n_wide + h * unit_pieces
                for p in range(first, first + unit_pieces):
                    pltpu.make_async_copy(panel.at[p], panel.at[p], recv_sem.at[p]).wait()
                left = panel[first : first + unit_pieces].reshape(unit_rows, width)
                bias = jnp.where(left[:, 0:1].astype(jnp.float32) < 2.0, -SCALE, NEVER)
                row_bias.append(bias)
                for b in range(k):
                    right = panel[b * n_wide : (b + 1) * n_wide].reshape(block, width)
                    e = jnp.exp2(rows_times_rows(left, right) * SCALE + bias + lane_bias[b])
                    down = jnp.sum(e, axis=0, keepdims=True)
                    if h == 0:
                        sums[b, k : k + 1, :] = down
                    else:
                        sums[b, k : k + 1, :] += down
                    folded = e[:, :128]
                    for lane in range(128, block, 128):
                        folded = folded + e[:, lane : lane + 128]
                    part[b, h * unit_rows : (h + 1) * unit_rows, :] = folded
            whole = panel[k * n_wide : (k + 1) * n_wide].reshape(block, width)
            valid = rows_times_rows(pick, whole[:, :128])[0:1] < 2.0
            lane_bias.append(jnp.where(valid, 0.0, NEVER))
            own_sum = jnp.zeros((1, block), jnp.float32)
            for h in range(HALVES):
                left = panel[
                    k * n_wide + h * unit_pieces : k * n_wide + (h + 1) * unit_pieces
                ].reshape(unit_rows, width)
                e = jnp.exp2(rows_times_rows(left, whole) * SCALE + row_bias[h] + lane_bias[k])
                own_sum = own_sum + jnp.sum(e, axis=0, keepdims=True)
            sums[k, k : k + 1, :] = own_sum
            sums[k, n_grp : n_grp + 1, :] = valid.astype(jnp.float32)
            for b in range(k):
                across = rows_times_rows(ones, part[b], lax.Precision.HIGHEST)
                sums[k, b : b + 1, :] = across[0:1]

        keep = pltpu.make_async_copy(sums.at[0], result, take_sem)
        keep.start()
        gives = []
        for k in range(1, n_grp):
            give = pltpu.make_async_remote_copy(
                src_ref=sums.at[k], dst_ref=result,
                send_sem=give_sem.at[k], recv_sem=take_sem,
                device_id=(me_wide, grp_of(k, parity)), device_id_type=MESH,
            )
            give.start()
            gives.append(give)
        for give in gives:
            give.wait_send()

    sooner = (
        lax.broadcasted_iota(jnp.int32, (block, block), 0)
        < lax.broadcasted_iota(jnp.int32, (block, block), 1)
    ).astype(jnp.float32).astype(jnp.bfloat16)
    position = lax.broadcasted_iota(jnp.int32, (block, block), 0)
    weights = []
    for k in range(n_grp):
        named = grp_of(k, parity)
        weight = jnp.float32(0.0)
        for p in range(pairs_ref.shape[0]):
            weight = weight + jnp.where(pairs_ref[p] == named, 1.0, 0.0)
        weights.append(weight)
    pltpu.make_async_copy(result, result, take_sem).wait()
    got = result[...]
    flags = got[n_grp : n_grp + 1]
    ahead = jnp.dot(
        jnp.broadcast_to(flags, (8, block)).astype(jnp.bfloat16), sooner,
        preferred_element_type=jnp.float32,
    )[0:1]
    slot_place = jnp.where(flags > 0.5, ahead, -1.0).astype(jnp.int32)
    squeeze = (position == slot_place).astype(jnp.float32)
    total = jnp.zeros((1, block), jnp.float32)
    for k in range(n_grp):
        total = total + got[k : k + 1] * weights[k]
    out_ref[...] = rows_times_rows(
        jnp.broadcast_to(total, (8, block)), squeeze, lax.Precision.HIGHEST
    )[0:1]

    for o in range(n_wide):
        @pl.when(jnp.logical_not(is_home & (me_wide == o)))
        def _():
            piece_copy(o).wait_send()


def gathered(embeds, bucket, pairs):
    n_wide, n_grp = lax.axis_size("wide"), lax.axis_size("grp")
    row_dev, width = embeds.shape
    cap = BLK // n_wide
    vmem = pl.BlockSpec(memory_space=pltpu.VMEM)
    return pl.pallas_call(
        functools.partial(gather_kernel, n_wide, n_grp, cap),
        out_shape=jax.ShapeDtypeStruct((1, BLK), jnp.float32),
        in_specs=[
            pl.BlockSpec(memory_space=pl.ANY), vmem, pl.BlockSpec(memory_space=pltpu.SMEM)
        ],
        out_specs=vmem,
        scratch_shapes=[
            pltpu.VMEM((row_dev, width), embeds.dtype),
            pltpu.VMEM((n_wide, cap, width), jnp.bfloat16),
            pltpu.VMEM((n_wide * n_grp, cap, width), jnp.bfloat16),
            pltpu.VMEM((n_grp, BLK, 128), jnp.float32),
            pltpu.VMEM((n_grp, 8, BLK), jnp.float32),
            pltpu.VMEM((8, BLK), jnp.float32),
            pltpu.SemaphoreType.DMA,
            pltpu.SemaphoreType.DMA((n_wide,)),
            pltpu.SemaphoreType.DMA((n_wide * n_grp,)),
            pltpu.SemaphoreType.DMA((n_grp,)),
            pltpu.SemaphoreType.DMA,
        ],
        compiler_params=pltpu.CompilerParams(
            collective_id=0, has_side_effects=True, vmem_limit_bytes=40 * 1024 * 1024
        ),
        cost_estimate=pl.CostEstimate(
            flops=20 * BLK * BLK * width, bytes_accessed=2 * row_dev * width,
            transcendentals=10 * BLK * BLK,
        ),
    )(embeds, bucket.reshape(1, row_dev), pairs)


def solution(mesh):
    n_wide, n_grp = mesh.shape["wide"], mesh.shape["grp"]
    if n_grp != 4 or (BLK // n_wide) % 16:
        return general(mesh)
    placed = (P(("wide", "grp"), None), P(("wide", "grp")), P(("wide", "grp")))
    return jax.shard_map(
        gathered, mesh=mesh, in_specs=placed, out_specs=P(("wide", "grp"), None), check_vma=False
    )
```

```python
import jax
import jax.numpy as jnp
from jax import lax
from jax.experimental import pallas as pl
from jax.experimental.pallas import tpu as pltpu
from jax.sharding import PartitionSpec as P
import functools
import math

BLK = 384


SHARPNESS = 10.0
EPSILON = 1e-06


def pair_sums(left_rows, right_rows, right_weight):
    cosines = lax.dot_general(
        left_rows, right_rows, (((1,), (1,)), ((), ())), preferred_element_type=jnp.float32
    )
    return jnp.sum(jnp.exp(SHARPNESS * (cosines - 1.0)) * right_weight[None, :], axis=1)


def per_device(embeds, bucket, pairs):
    wide_count = lax.axis_size("wide")
    feature_width = embeds.shape[1]
    capacity = BLK // wide_count
    floats = embeds.astype(jnp.float32)
    unit_rows = (
        floats * lax.rsqrt(jnp.sum(floats * floats, axis=1, keepdims=True) + EPSILON)
    ).astype(jnp.bfloat16)
    onehot = (bucket[:, None] == jnp.arange(wide_count, dtype=jnp.int32)[None, :]).astype(jnp.int32)
    row_ranks = jnp.sum(jnp.cumsum(onehot, axis=0) * onehot, axis=1) - 1
    counts = jnp.sum(onehot, axis=0)
    send_slots = bucket * capacity + row_ranks
    outgoing = (
        jnp.zeros((wide_count * capacity, feature_width), jnp.bfloat16)
        .at[send_slots]
        .set(unit_rows)
    )
    received, arrived = (
        lax.all_to_all(
            outgoing.reshape(wide_count, capacity, feature_width),
            "wide",
            split_axis=0,
            concat_axis=0,
            tiled=True,
        ),
        lax.all_to_all(
            counts.reshape(wide_count, 1), "wide", split_axis=0, concat_axis=0, tiled=True
        ),
    )
    arrived = arrived.reshape(wide_count)
    offsets = jnp.cumsum(arrived) - arrived
    within = jnp.arange(capacity, dtype=jnp.int32)
    places = jnp.where(within[None, :] < arrived[:, None], offsets[:, None] + within[None, :], BLK)
    own_block = (
        jnp.zeros((BLK, feature_width), jnp.bfloat16)
        .at[places.reshape(-1)]
        .set(received.reshape(wide_count * capacity, feature_width), mode="drop")
    )
    total_rows = jnp.sum(arrived)
    valid_rows = (jnp.arange(BLK, dtype=jnp.int32) < total_rows).astype(jnp.float32)
    flags_wire = valid_rows.astype(jnp.bfloat16)
    live_count = jnp.sum((pairs >= 0).astype(jnp.int32))
    first_row = jnp.int32(0)
    panel_rows = lax.all_gather(own_block, "grp", axis=0, tiled=True)
    panel_flags = lax.all_gather(flags_wire, "grp", axis=0, tiled=True)
    length = panel_rows.shape[0]
    span_rows = min(BLK, length)

    def add_pair(pair_index, running_sum):
        target = pairs[pair_index] * BLK
        shift_rows = jnp.clip(target, 0, length - span_rows)

        def add_tile(before):
            right_rows = lax.dynamic_slice_in_dim(panel_rows, shift_rows, span_rows, 0)
            right_flags = lax.dynamic_slice_in_dim(panel_flags, shift_rows, span_rows, 0).astype(
                jnp.float32
            )
            global_rows = shift_rows + jnp.arange(span_rows, dtype=jnp.int32)
            inside = (global_rows >= target) & (global_rows < target + BLK)
            return before + pair_sums(own_block, right_rows, jnp.where(inside, right_flags, 0.0))

        touches = (target < first_row + length) & (target + BLK > first_row)
        return lax.cond(touches, add_tile, lambda before: before, running_sum)

    density = lax.fori_loop(0, live_count, add_pair, jnp.zeros((BLK,), jnp.float32))
    return (density * valid_rows).reshape(1, BLK)


def general(mesh):
    placed = (P(("wide", "grp"), None), P(("wide", "grp")), P(("wide", "grp")))
    return jax.shard_map(
        per_device, mesh=mesh, in_specs=placed, out_specs=P(("wide", "grp"), None), check_vma=False
    )


MESH = pl.DeviceIdType.MESH
SCALE = SHARPNESS * math.log2(math.e)
NEVER = -1e30
MARK = 4.0


def rows_times_rows(left, right, precision=None):
    return lax.dot_general(
        left, right, (((1,), (1,)), ((), ())), precision=precision,
        preferred_element_type=jnp.float32,
    )


def thirds(values, axis):
    high = values.astype(jnp.bfloat16)
    rest = values - high.astype(jnp.float32)
    middle = rest.astype(jnp.bfloat16)
    low = (rest - middle.astype(jnp.float32)).astype(jnp.bfloat16)
    return jnp.concatenate([high, middle, low], axis=axis)


def gather_kernel(
    n_wide, n_grp, cap, embeds_ref, bucket_ref, pairs_ref, out_ref,
    rows, bucket_row, entries, outgoing, panel, sums, result,
    load_sem, send_sem, recv_sem, give_sem, take_sem,
):
    me_wide, me_grp = lax.axis_index("wide"), lax.axis_index("grp")
    parity = lax.rem(me_wide, 2)
    my_home = n_grp // 2 - parity
    is_home = me_grp == my_home
    row_dev, width = rows.shape
    block = n_wide * cap
    devices = n_wide * n_grp
    half = n_wide // 2

    def order_of(grp, odd):
        along = grp + odd * (n_grp - 1 - 2 * grp)
        return jnp.where(along >= n_grp // 2, along - n_grp // 2, n_grp - 1 - along)

    def grp_of(order, odd):
        along = order + n_grp // 2 if order < n_grp // 2 else n_grp - 1 - order
        return along + odd * (n_grp - 1 - 2 * along)

    load = pltpu.make_async_copy(embeds_ref, rows, load_sem.at[0])
    load.start()
    load_bucket = pltpu.make_async_copy(bucket_ref, bucket_row, load_sem.at[1])
    load_bucket.start()
    load_pairs = pltpu.make_async_copy(pairs_ref, entries, load_sem.at[2])
    load_pairs.start()
    barrier = pltpu.get_barrier_semaphore()

    @pl.when(is_home)
    def _():
        def greet(step, carry):
            other = lax.rem(me_wide * n_grp + me_grp + step, devices)
            pl.semaphore_signal(
                barrier, inc=1, device_id=(other // n_grp, lax.rem(other, n_grp)),
                device_id_type=MESH,
            )
            return carry

        lax.fori_loop(1, devices, greet, 0)

    @pl.when(jnp.logical_not(is_home))
    def _():
        pl.semaphore_signal(
            barrier, inc=1, device_id=(me_wide, my_home), device_id_type=MESH
        )

    load_bucket.wait()
    bucket = bucket_row[...].reshape(1, row_dev)
    of_bucket = lax.broadcasted_iota(jnp.int32, (n_wide, row_dev), 0) == bucket
    onehot = of_bucket.astype(jnp.float32)
    earlier = (
        lax.broadcasted_iota(jnp.int32, (row_dev, row_dev), 0)
        < lax.broadcasted_iota(jnp.int32, (row_dev, row_dev), 1)
    ).astype(jnp.float32).astype(jnp.bfloat16)
    before = jnp.dot(onehot.astype(jnp.bfloat16), earlier, preferred_element_type=jnp.float32)
    rank = jnp.sum(before * onehot, axis=0, keepdims=True).astype(jnp.int32)
    counts = jnp.sum(onehot, axis=1, keepdims=True).astype(jnp.int32)
    slots = (bucket >> 1) * cap + rank

    load.wait()
    floats = rows[...].astype(jnp.float32)
    unit = (
        floats * lax.rsqrt(jnp.sum(floats * floats, axis=1, keepdims=True) + EPSILON)
    ).astype(jnp.bfloat16)
    first_lane = lax.broadcasted_iota(jnp.int32, (cap, 128), 1) == 0
    within = lax.broadcasted_iota(jnp.int32, (cap, 128), 0)

    odd_of = [1 - lax.rem(me_grp, 2), lax.rem(me_grp, 2)]

    def fill(turn):
        odd = odd_of[turn]
        mine = jnp.where((bucket & 1) == odd, slots, -1)
        chosen = (
            lax.broadcasted_iota(jnp.int32, (half * cap, row_dev), 0) == mine
        ).astype(jnp.float32).astype(jnp.bfloat16)
        placed = jnp.dot(chosen, unit, preferred_element_type=jnp.float32)
        for m in range(half):
            piece = placed[m * cap : (m + 1) * cap]
            held = jnp.where(odd == 0, counts[2 * m : 2 * m + 1], counts[2 * m + 1 : 2 * m + 2])
            padding = first_lane & (within >= held)
            at = turn * half + m
            outgoing[at, :, :128] = jnp.where(padding, MARK, piece[:, :128]).astype(jnp.bfloat16)
            outgoing[at, :, 128:] = piece[:, 128:].astype(jnp.bfloat16)

    def piece_copy(turn, step):
        odd = odd_of[turn]
        m = lax.rem(me_wide // 2 + step, half)
        place = order_of(me_grp, odd) * n_wide + me_wide
        return pltpu.make_async_remote_copy(
            src_ref=outgoing.at[turn * half + m],
            dst_ref=panel.at[pl.ds(pl.multiple_of(place * cap, cap), cap)],
            send_sem=send_sem.at[turn * half + m], recv_sem=recv_sem.at[place],
            device_id=(2 * m + odd, n_grp // 2 - odd), device_id_type=MESH,
        )

    fill(0)

    @pl.when(is_home)
    def _():
        pl.semaphore_wait(barrier, n_wide - 1 + n_grp - 1)

    @pl.when(jnp.logical_not(is_home))
    def _():
        pl.semaphore_wait(barrier, n_wide)

    for step in range(half):
        piece_copy(0, step).start()
    fill(1)

    is_end = (me_grp == 0) | (me_grp == n_grp - 1)

    @pl.when(is_end)
    def _():
        for step in range(half):
            piece_copy(0, step).wait_send()
            piece_copy(1, step).start()

    @pl.when(jnp.logical_not(is_end))
    def _():
        for step in range(1, half):
            piece_copy(1, step).start()

        @pl.when(jnp.logical_not(is_home))
        def _():
            piece_copy(1, 0).start()

    def arrive(place):
        slot = panel.at[place * cap : (place + 1) * cap]
        pltpu.make_async_copy(slot, slot, recv_sem.at[place]).wait()

    @pl.when(is_home)
    def _():
        place = order_of(me_grp, parity) * n_wide + me_wide
        pltpu.make_async_copy(
            outgoing.at[half + me_wide // 2],
            panel.at[pl.ds(pl.multiple_of(place * cap, cap), cap)],
            recv_sem.at[place],
        ).start()
        pick = (
            (lax.broadcasted_iota(jnp.int32, (8, 128), 1) == 0)
            .astype(jnp.float32).astype(jnp.bfloat16)
        )
        ones = jnp.ones((8, 3 * 128), jnp.bfloat16)

        def lane_flags(first, count):
            return rows_times_rows(pick, panel[first : first + count, :128])[0:1] < 2.0

        def fold(e, lanes):
            folded = e[:, :128]
            for lane in range(128, lanes, 128):
                folded = folded + e[:, lane : lane + 128]
            return folded

        def row_sums(folded):
            return rows_times_rows(ones, thirds(folded, 1))[0:1]

        lane_bias = []
        for k in range(n_grp):
            base = k * block
            step_rows = 128 if k == n_grp - 1 else block
            own_bias = []
            arrived = 0
            for start in range(0, block, step_rows):
                stop = start + step_rows
                while arrived * cap < stop:
                    arrive(k * n_wide + arrived)
                    arrived += 1
                left = panel[base + start : base + stop]
                bias = jnp.where(left[:, 0:1].astype(jnp.float32) < 2.0, -SCALE, NEVER)
                valid = lane_flags(base + start, step_rows)
                sums[k, n_grp : n_grp + 1, start:stop] = valid.astype(jnp.float32)
                own_bias.append(jnp.where(valid, 0.0, NEVER))
                for b in range(k):
                    right = panel[b * block : (b + 1) * block]
                    e = jnp.exp2(rows_times_rows(left, right) * SCALE + bias + lane_bias[b])
                    down = jnp.sum(e, axis=0, keepdims=True)
                    if start == 0:
                        sums[b, k : k + 1, :] = down
                    else:
                        sums[b, k : k + 1, :] += down
                    sums[k, b : b + 1, start:stop] = row_sums(fold(e, block))
                right = panel[base : base + stop]
                e = jnp.exp2(
                    rows_times_rows(left, right) * SCALE + bias
                    + jnp.concatenate(own_bias, axis=1)
                )
                down = jnp.sum(e, axis=0, keepdims=True)
                if start == 0:
                    sums[k, k : k + 1, start:stop] = down
                else:
                    sums[k, k : k + 1, :start] += down[:, :start]
                    sums[k, k : k + 1, start:stop] = down[:, start:] + row_sums(fold(e, start))
            lane_bias.append(jnp.concatenate(own_bias, axis=1))

        keep = pltpu.make_async_copy(sums.at[0], result, take_sem)
        keep.start()
        gives = []
        for k in range(1, n_grp):
            give = pltpu.make_async_remote_copy(
                src_ref=sums.at[k], dst_ref=result,
                send_sem=give_sem.at[k], recv_sem=take_sem,
                device_id=(me_wide, grp_of(k, parity)), device_id_type=MESH,
            )
            give.start()
            gives.append(give)
        for give in gives:
            give.wait_send()

    sooner = (
        lax.broadcasted_iota(jnp.int32, (block, block), 0)
        < lax.broadcasted_iota(jnp.int32, (block, block), 1)
    ).astype(jnp.float32).astype(jnp.bfloat16)
    position = lax.broadcasted_iota(jnp.int32, (block, block), 0)
    load_pairs.wait()
    weights = []
    for k in range(n_grp):
        named = grp_of(k, parity)
        weight = jnp.float32(0.0)
        for p in range(entries.shape[0]):
            weight = weight + jnp.where(entries[p] == named, 1.0, 0.0)
        weights.append(weight)
    pltpu.make_async_copy(result, result, take_sem).wait()
    got = result[...]
    flags = got[n_grp : n_grp + 1]
    ahead = jnp.dot(
        jnp.broadcast_to(flags, (8, block)).astype(jnp.bfloat16), sooner,
        preferred_element_type=jnp.float32,
    )[0:1]
    slot_place = jnp.where(flags > 0.5, ahead, -1.0).astype(jnp.int32)
    squeeze = (position == slot_place).astype(jnp.float32).astype(jnp.bfloat16)
    total = jnp.zeros((1, block), jnp.float32)
    for k in range(n_grp):
        total = total + got[k : k + 1] * weights[k]
    squeezed = rows_times_rows(
        thirds(jnp.broadcast_to(total, (16, block)), 0), squeeze
    )
    out_ref[...] = squeezed[0:1] + squeezed[16:17] + squeezed[32:33]

    for step in range(half):
        @pl.when(jnp.logical_not(is_end))
        def _():
            piece_copy(0, step).wait_send()

        @pl.when(jnp.logical_not(is_home & (step == 0)))
        def _():
            piece_copy(1, step).wait_send()


def gathered(embeds, bucket, pairs):
    n_wide, n_grp = lax.axis_size("wide"), lax.axis_size("grp")
    row_dev, width = embeds.shape
    cap = BLK // n_wide
    return pl.pallas_call(
        functools.partial(gather_kernel, n_wide, n_grp, cap),
        out_shape=jax.ShapeDtypeStruct((1, BLK), jnp.float32),
        in_specs=[pl.BlockSpec(memory_space=pl.ANY)] * 3,
        out_specs=pl.BlockSpec(memory_space=pltpu.VMEM),
        scratch_shapes=[
            pltpu.VMEM((row_dev, width), embeds.dtype),
            pltpu.VMEM((row_dev,), jnp.int32),
            pltpu.SMEM(pairs.shape, jnp.int32),
            pltpu.VMEM((n_wide, cap, width), jnp.bfloat16),
            pltpu.VMEM((n_grp * BLK, width), jnp.bfloat16),
            pltpu.VMEM((n_grp, 8, BLK), jnp.float32),
            pltpu.VMEM((8, BLK), jnp.float32),
            pltpu.SemaphoreType.DMA((3,)),
            pltpu.SemaphoreType.DMA((n_wide,)),
            pltpu.SemaphoreType.DMA((n_wide * n_grp,)),
            pltpu.SemaphoreType.DMA((n_grp,)),
            pltpu.SemaphoreType.DMA,
        ],
        compiler_params=pltpu.CompilerParams(
            collective_id=0, has_side_effects=True, vmem_limit_bytes=60 * 1024 * 1024
        ),
        cost_estimate=pl.CostEstimate(
            flops=20 * BLK * BLK * width, bytes_accessed=2 * row_dev * width,
            transcendentals=10 * BLK * BLK,
        ),
    )(embeds, bucket, pairs)


def solution(mesh):
    n_wide, n_grp = mesh.shape["wide"], mesh.shape["grp"]
    if n_grp != 4 or (BLK // n_wide) % 16:
        return general(mesh)
    placed = (P(("wide", "grp"), None), P(("wide", "grp")), P(("wide", "grp")))
    return jax.shard_map(
        gathered, mesh=mesh, in_specs=placed, out_specs=P(("wide", "grp"), None), check_vma=False
    )
```

```python
import jax
import jax.numpy as jnp
from jax import lax
from jax.experimental import pallas as pl
from jax.experimental.pallas import tpu as pltpu
from jax.sharding import PartitionSpec as P
import functools
import math

BLK = 384


SHARPNESS = 10.0
EPSILON = 1e-06


def pair_sums(left_rows, right_rows, right_weight):
    cosines = lax.dot_general(
        left_rows, right_rows, (((1,), (1,)), ((), ())), preferred_element_type=jnp.float32
    )
    return jnp.sum(jnp.exp(SHARPNESS * (cosines - 1.0)) * right_weight[None, :], axis=1)


def per_device(embeds, bucket, pairs):
    wide_count = lax.axis_size("wide")
    feature_width = embeds.shape[1]
    capacity = BLK // wide_count
    floats = embeds.astype(jnp.float32)
    unit_rows = (
        floats * lax.rsqrt(jnp.sum(floats * floats, axis=1, keepdims=True) + EPSILON)
    ).astype(jnp.bfloat16)
    onehot = (bucket[:, None] == jnp.arange(wide_count, dtype=jnp.int32)[None, :]).astype(jnp.int32)
    row_ranks = jnp.sum(jnp.cumsum(onehot, axis=0) * onehot, axis=1) - 1
    counts = jnp.sum(onehot, axis=0)
    send_slots = bucket * capacity + row_ranks
    outgoing = (
        jnp.zeros((wide_count * capacity, feature_width), jnp.bfloat16)
        .at[send_slots]
        .set(unit_rows)
    )
    received, arrived = (
        lax.all_to_all(
            outgoing.reshape(wide_count, capacity, feature_width),
            "wide",
            split_axis=0,
            concat_axis=0,
            tiled=True,
        ),
        lax.all_to_all(
            counts.reshape(wide_count, 1), "wide", split_axis=0, concat_axis=0, tiled=True
        ),
    )
    arrived = arrived.reshape(wide_count)
    offsets = jnp.cumsum(arrived) - arrived
    within = jnp.arange(capacity, dtype=jnp.int32)
    places = jnp.where(within[None, :] < arrived[:, None], offsets[:, None] + within[None, :], BLK)
    own_block = (
        jnp.zeros((BLK, feature_width), jnp.bfloat16)
        .at[places.reshape(-1)]
        .set(received.reshape(wide_count * capacity, feature_width), mode="drop")
    )
    total_rows = jnp.sum(arrived)
    valid_rows = (jnp.arange(BLK, dtype=jnp.int32) < total_rows).astype(jnp.float32)
    flags_wire = valid_rows.astype(jnp.bfloat16)
    live_count = jnp.sum((pairs >= 0).astype(jnp.int32))
    first_row = jnp.int32(0)
    panel_rows = lax.all_gather(own_block, "grp", axis=0, tiled=True)
    panel_flags = lax.all_gather(flags_wire, "grp", axis=0, tiled=True)
    length = panel_rows.shape[0]
    span_rows = min(BLK, length)

    def add_pair(pair_index, running_sum):
        target = pairs[pair_index] * BLK
        shift_rows = jnp.clip(target, 0, length - span_rows)

        def add_tile(before):
            right_rows = lax.dynamic_slice_in_dim(panel_rows, shift_rows, span_rows, 0)
            right_flags = lax.dynamic_slice_in_dim(panel_flags, shift_rows, span_rows, 0).astype(
                jnp.float32
            )
            global_rows = shift_rows + jnp.arange(span_rows, dtype=jnp.int32)
            inside = (global_rows >= target) & (global_rows < target + BLK)
            return before + pair_sums(own_block, right_rows, jnp.where(inside, right_flags, 0.0))

        touches = (target < first_row + length) & (target + BLK > first_row)
        return lax.cond(touches, add_tile, lambda before: before, running_sum)

    density = lax.fori_loop(0, live_count, add_pair, jnp.zeros((BLK,), jnp.float32))
    return (density * valid_rows).reshape(1, BLK)


def general(mesh):
    placed = (P(("wide", "grp"), None), P(("wide", "grp")), P(("wide", "grp")))
    return jax.shard_map(
        per_device, mesh=mesh, in_specs=placed, out_specs=P(("wide", "grp"), None), check_vma=False
    )


MESH = pl.DeviceIdType.MESH
SCALE = SHARPNESS * math.log2(math.e)
NEVER = -1e30
MARK = 4.0


def rows_times_rows(left, right, precision=None):
    return lax.dot_general(
        left, right, (((1,), (1,)), ((), ())), precision=precision,
        preferred_element_type=jnp.float32,
    )


def thirds(values, axis):
    high = values.astype(jnp.bfloat16)
    rest = values - high.astype(jnp.float32)
    middle = rest.astype(jnp.bfloat16)
    low = (rest - middle.astype(jnp.float32)).astype(jnp.bfloat16)
    return jnp.concatenate([high, middle, low], axis=axis)


def gather_kernel(
    n_wide, n_grp, cap, embeds_ref, bucket_ref, pairs_ref, out_ref,
    rows, bucket_row, entries, outgoing, panel, sums, result,
    load_sem, send_sem, recv_sem, give_sem, take_sem,
):
    me_wide, me_grp = lax.axis_index("wide"), lax.axis_index("grp")
    parity = lax.rem(me_wide, 2)
    my_home = n_grp // 2 - parity
    is_home = me_grp == my_home
    row_dev, width = rows.shape
    block = n_wide * cap
    devices = n_wide * n_grp
    half = n_wide // 2

    def order_of(grp, odd):
        along = grp + odd * (n_grp - 1 - 2 * grp)
        return jnp.where(along >= n_grp // 2, along - n_grp // 2, n_grp - 1 - along)

    def grp_of(order, odd):
        along = order + n_grp // 2 if order < n_grp // 2 else n_grp - 1 - order
        return along + odd * (n_grp - 1 - 2 * along)

    load = pltpu.make_async_copy(embeds_ref, rows, load_sem.at[0])
    load.start()
    load_bucket = pltpu.make_async_copy(bucket_ref, bucket_row, load_sem.at[1])
    load_bucket.start()
    load_pairs = pltpu.make_async_copy(pairs_ref, entries, load_sem.at[2])
    load_pairs.start()
    barrier = pltpu.get_barrier_semaphore()

    @pl.when(is_home)
    def _():
        def greet(step, carry):
            other = lax.rem(me_wide * n_grp + me_grp + step, devices)
            pl.semaphore_signal(
                barrier, inc=1, device_id=(other // n_grp, lax.rem(other, n_grp)),
                device_id_type=MESH,
            )
            return carry

        lax.fori_loop(1, devices, greet, 0)

    @pl.when(jnp.logical_not(is_home))
    def _():
        pl.semaphore_signal(
            barrier, inc=1, device_id=(me_wide, my_home), device_id_type=MESH
        )

    load_bucket.wait()
    bucket = bucket_row[...].reshape(1, row_dev)
    of_bucket = lax.broadcasted_iota(jnp.int32, (n_wide, row_dev), 0) == bucket
    onehot = of_bucket.astype(jnp.float32)
    earlier = (
        lax.broadcasted_iota(jnp.int32, (row_dev, row_dev), 0)
        < lax.broadcasted_iota(jnp.int32, (row_dev, row_dev), 1)
    ).astype(jnp.float32).astype(jnp.bfloat16)
    before = jnp.dot(onehot.astype(jnp.bfloat16), earlier, preferred_element_type=jnp.float32)
    rank = jnp.sum(before * onehot, axis=0, keepdims=True).astype(jnp.int32)
    counts = jnp.sum(onehot, axis=1, keepdims=True).astype(jnp.int32)
    slots = (bucket >> 1) * cap + rank

    load.wait()
    floats = rows[...].astype(jnp.float32)
    unit = (
        floats * lax.rsqrt(jnp.sum(floats * floats, axis=1, keepdims=True) + EPSILON)
    ).astype(jnp.bfloat16)
    first_lane = lax.broadcasted_iota(jnp.int32, (cap, 128), 1) == 0
    within = lax.broadcasted_iota(jnp.int32, (cap, 128), 0)

    odd_of = [1 - lax.rem(me_grp, 2), lax.rem(me_grp, 2)]

    def fill(turn):
        odd = odd_of[turn]
        mine = jnp.where((bucket & 1) == odd, slots, -1)
        chosen = (
            lax.broadcasted_iota(jnp.int32, (half * cap, row_dev), 0) == mine
        ).astype(jnp.float32).astype(jnp.bfloat16)
        placed = jnp.dot(chosen, unit, preferred_element_type=jnp.float32)
        for m in range(half):
            piece = placed[m * cap : (m + 1) * cap]
            held = jnp.where(odd == 0, counts[2 * m : 2 * m + 1], counts[2 * m + 1 : 2 * m + 2])
            padding = first_lane & (within >= held)
            at = turn * half + m
            outgoing[at, :, :128] = jnp.where(padding, MARK, piece[:, :128]).astype(jnp.bfloat16)
            outgoing[at, :, 128:] = piece[:, 128:].astype(jnp.bfloat16)

    def piece_copy(turn, step):
        odd = odd_of[turn]
        m = lax.rem(me_wide // 2 + step, half)
        place = order_of(me_grp, odd) * n_wide + 2 * step + parity
        return pltpu.make_async_remote_copy(
            src_ref=outgoing.at[turn * half + m],
            dst_ref=panel.at[pl.ds(pl.multiple_of(place * cap, cap), cap)],
            send_sem=send_sem.at[turn * half + m], recv_sem=recv_sem.at[place],
            device_id=(2 * m + odd, n_grp // 2 - odd), device_id_type=MESH,
        )

    fill(0)

    @pl.when(is_home)
    def _():
        pl.semaphore_wait(barrier, n_wide - 1 + n_grp - 1)

    @pl.when(jnp.logical_not(is_home))
    def _():
        pl.semaphore_wait(barrier, n_wide)

    for step in range(half):
        piece_copy(0, step).start()
    fill(1)

    is_end = (me_grp == 0) | (me_grp == n_grp - 1)

    @pl.when(is_end)
    def _():
        for step in range(half):
            piece_copy(0, step).wait_send()
            piece_copy(1, step).start()

    @pl.when(jnp.logical_not(is_end))
    def _():
        for step in range(1, half):
            piece_copy(1, step).start()

        @pl.when(jnp.logical_not(is_home))
        def _():
            piece_copy(1, 0).start()

    def shard_order(axis):
        slot = lax.broadcasted_iota(jnp.int32, (block, block), axis)
        mine = me_wide // 2
        step = jnp.zeros((block, block), jnp.int32)
        for t in range(1, half):
            step = step + (slot >= 2 * t * cap).astype(jnp.int32)
        wraps = (step > mine).astype(jnp.int32)
        return slot + cap * (2 * mine - 4 * step + n_wide * wraps)

    sooner = (shard_order(0) < shard_order(1)).astype(jnp.float32).astype(jnp.bfloat16)
    load_pairs.wait()
    weights = []
    for k in range(n_grp):
        named = grp_of(k, parity)
        weight = jnp.float32(0.0)
        for p in range(entries.shape[0]):
            weight = weight + jnp.where(entries[p] == named, 1.0, 0.0)
        weights.append(weight)

    def arrive(place):
        slot = panel.at[place * cap : (place + 1) * cap]
        pltpu.make_async_copy(slot, slot, recv_sem.at[place]).wait()

    @pl.when(is_home)
    def _():
        place = order_of(me_grp, parity) * n_wide + parity
        pltpu.make_async_copy(
            outgoing.at[half + me_wide // 2],
            panel.at[pl.ds(pl.multiple_of(place * cap, cap), cap)],
            recv_sem.at[place],
        ).start()
        pick = (
            (lax.broadcasted_iota(jnp.int32, (8, 128), 1) == 0)
            .astype(jnp.float32).astype(jnp.bfloat16)
        )
        ones = jnp.ones((8, 3 * 128), jnp.bfloat16)

        def lane_flags(first, count):
            return rows_times_rows(pick, panel[first : first + count, :128])[0:1] < 2.0

        def fold(e, lanes):
            folded = e[:, :128]
            for lane in range(128, lanes, 128):
                folded = folded + e[:, lane : lane + 128]
            return folded

        def row_sums(folded):
            return rows_times_rows(ones, thirds(folded, 1))[0:1]

        lane_bias = []
        for k in range(n_grp):
            base = k * block
            step_rows = 128 if k == n_grp - 1 else block
            own_bias = []
            arrived = 0
            for start in range(0, block, step_rows):
                stop = start + step_rows
                while arrived * cap < stop:
                    arrive(k * n_wide + arrived)
                    arrived += 1
                left = panel[base + start : base + stop]
                bias = jnp.where(left[:, 0:1].astype(jnp.float32) < 2.0, -SCALE, NEVER)
                valid = lane_flags(base + start, step_rows)
                sums[k, n_grp : n_grp + 1, start:stop] = valid.astype(jnp.float32)
                own_bias.append(jnp.where(valid, 0.0, NEVER))
                for b in range(k):
                    right = panel[b * block : (b + 1) * block]
                    e = jnp.exp2(rows_times_rows(left, right) * SCALE + bias + lane_bias[b])
                    down = jnp.sum(e, axis=0, keepdims=True)
                    if start == 0:
                        sums[b, k : k + 1, :] = down
                    else:
                        sums[b, k : k + 1, :] += down
                    sums[k, b : b + 1, start:stop] = row_sums(fold(e, block))
                right = panel[base : base + stop]
                e = jnp.exp2(
                    rows_times_rows(left, right) * SCALE + bias
                    + jnp.concatenate(own_bias, axis=1)
                )
                down = jnp.sum(e, axis=0, keepdims=True)
                if start == 0:
                    sums[k, k : k + 1, start:stop] = down
                else:
                    sums[k, k : k + 1, :start] += down[:, :start]
                    sums[k, k : k + 1, start:stop] = down[:, start:] + row_sums(fold(e, start))
            lane_bias.append(jnp.concatenate(own_bias, axis=1))

        keep = pltpu.make_async_copy(sums.at[0], result, take_sem)
        keep.start()
        gives = []
        for k in range(1, n_grp):
            give = pltpu.make_async_remote_copy(
                src_ref=sums.at[k], dst_ref=result,
                send_sem=give_sem.at[k], recv_sem=take_sem,
                device_id=(me_wide, grp_of(k, parity)), device_id_type=MESH,
            )
            give.start()
            gives.append(give)
        for give in gives:
            give.wait_send()

    pltpu.make_async_copy(result, result, take_sem).wait()
    got = result[...]
    flags = got[n_grp : n_grp + 1]
    ahead = jnp.dot(
        jnp.broadcast_to(flags, (8, block)).astype(jnp.bfloat16), sooner,
        preferred_element_type=jnp.float32,
    )[0:1]
    slot_place = jnp.where(flags > 0.5, ahead, -1.0).astype(jnp.int32)
    position = lax.broadcasted_iota(jnp.int32, (block, block), 0)
    squeeze = (position == slot_place).astype(jnp.float32).astype(jnp.bfloat16)
    total = jnp.zeros((1, block), jnp.float32)
    for k in range(n_grp):
        total = total + got[k : k + 1] * weights[k]
    squeezed = rows_times_rows(
        thirds(jnp.broadcast_to(total, (16, block)), 0), squeeze
    )
    out_ref[...] = squeezed[0:1] + squeezed[16:17] + squeezed[32:33]

    for step in range(half):
        @pl.when(jnp.logical_not(is_end))
        def _():
            piece_copy(0, step).wait_send()

        @pl.when(jnp.logical_not(is_home & (step == 0)))
        def _():
            piece_copy(1, step).wait_send()


def gathered(embeds, bucket, pairs):
    n_wide, n_grp = lax.axis_size("wide"), lax.axis_size("grp")
    row_dev, width = embeds.shape
    cap = BLK // n_wide
    return pl.pallas_call(
        functools.partial(gather_kernel, n_wide, n_grp, cap),
        out_shape=jax.ShapeDtypeStruct((1, BLK), jnp.float32),
        in_specs=[pl.BlockSpec(memory_space=pl.ANY)] * 3,
        out_specs=pl.BlockSpec(memory_space=pltpu.VMEM),
        scratch_shapes=[
            pltpu.VMEM((row_dev, width), embeds.dtype),
            pltpu.VMEM((row_dev,), jnp.int32),
            pltpu.SMEM(pairs.shape, jnp.int32),
            pltpu.VMEM((n_wide, cap, width), jnp.bfloat16),
            pltpu.VMEM((n_grp * BLK, width), jnp.bfloat16),
            pltpu.VMEM((n_grp, 8, BLK), jnp.float32),
            pltpu.VMEM((8, BLK), jnp.float32),
            pltpu.SemaphoreType.DMA((3,)),
            pltpu.SemaphoreType.DMA((n_wide,)),
            pltpu.SemaphoreType.DMA((n_wide * n_grp,)),
            pltpu.SemaphoreType.DMA((n_grp,)),
            pltpu.SemaphoreType.DMA,
        ],
        compiler_params=pltpu.CompilerParams(
            collective_id=0, has_side_effects=True, vmem_limit_bytes=60 * 1024 * 1024
        ),
        cost_estimate=pl.CostEstimate(
            flops=20 * BLK * BLK * width, bytes_accessed=2 * row_dev * width,
            transcendentals=10 * BLK * BLK,
        ),
    )(embeds, bucket, pairs)


def solution(mesh):
    n_wide, n_grp = mesh.shape["wide"], mesh.shape["grp"]
    if n_grp != 4 or (BLK // n_wide) % 16:
        return general(mesh)
    placed = (P(("wide", "grp"), None), P(("wide", "grp")), P(("wide", "grp")))
    return jax.shard_map(
        gathered, mesh=mesh, in_specs=placed, out_specs=P(("wide", "grp"), None), check_vma=False
    )
```

```python
import jax
import jax.numpy as jnp
from jax import lax
from jax.experimental import pallas as pl
from jax.experimental.pallas import tpu as pltpu
from jax.sharding import PartitionSpec as P
import functools
import math

BLK = 384


SHARPNESS = 10.0
EPSILON = 1e-06


def pair_sums(left_rows, right_rows, right_weight):
    cosines = lax.dot_general(
        left_rows, right_rows, (((1,), (1,)), ((), ())), preferred_element_type=jnp.float32
    )
    return jnp.sum(jnp.exp(SHARPNESS * (cosines - 1.0)) * right_weight[None, :], axis=1)


def per_device(embeds, bucket, pairs):
    wide_count = lax.axis_size("wide")
    feature_width = embeds.shape[1]
    capacity = BLK // wide_count
    floats = embeds.astype(jnp.float32)
    unit_rows = (
        floats * lax.rsqrt(jnp.sum(floats * floats, axis=1, keepdims=True) + EPSILON)
    ).astype(jnp.bfloat16)
    onehot = (bucket[:, None] == jnp.arange(wide_count, dtype=jnp.int32)[None, :]).astype(jnp.int32)
    row_ranks = jnp.sum(jnp.cumsum(onehot, axis=0) * onehot, axis=1) - 1
    counts = jnp.sum(onehot, axis=0)
    send_slots = bucket * capacity + row_ranks
    outgoing = (
        jnp.zeros((wide_count * capacity, feature_width), jnp.bfloat16)
        .at[send_slots]
        .set(unit_rows)
    )
    received, arrived = (
        lax.all_to_all(
            outgoing.reshape(wide_count, capacity, feature_width),
            "wide",
            split_axis=0,
            concat_axis=0,
            tiled=True,
        ),
        lax.all_to_all(
            counts.reshape(wide_count, 1), "wide", split_axis=0, concat_axis=0, tiled=True
        ),
    )
    arrived = arrived.reshape(wide_count)
    offsets = jnp.cumsum(arrived) - arrived
    within = jnp.arange(capacity, dtype=jnp.int32)
    places = jnp.where(within[None, :] < arrived[:, None], offsets[:, None] + within[None, :], BLK)
    own_block = (
        jnp.zeros((BLK, feature_width), jnp.bfloat16)
        .at[places.reshape(-1)]
        .set(received.reshape(wide_count * capacity, feature_width), mode="drop")
    )
    total_rows = jnp.sum(arrived)
    valid_rows = (jnp.arange(BLK, dtype=jnp.int32) < total_rows).astype(jnp.float32)
    flags_wire = valid_rows.astype(jnp.bfloat16)
    live_count = jnp.sum((pairs >= 0).astype(jnp.int32))
    first_row = jnp.int32(0)
    panel_rows = lax.all_gather(own_block, "grp", axis=0, tiled=True)
    panel_flags = lax.all_gather(flags_wire, "grp", axis=0, tiled=True)
    length = panel_rows.shape[0]
    span_rows = min(BLK, length)

    def add_pair(pair_index, running_sum):
        target = pairs[pair_index] * BLK
        shift_rows = jnp.clip(target, 0, length - span_rows)

        def add_tile(before):
            right_rows = lax.dynamic_slice_in_dim(panel_rows, shift_rows, span_rows, 0)
            right_flags = lax.dynamic_slice_in_dim(panel_flags, shift_rows, span_rows, 0).astype(
                jnp.float32
            )
            global_rows = shift_rows + jnp.arange(span_rows, dtype=jnp.int32)
            inside = (global_rows >= target) & (global_rows < target + BLK)
            return before + pair_sums(own_block, right_rows, jnp.where(inside, right_flags, 0.0))

        touches = (target < first_row + length) & (target + BLK > first_row)
        return lax.cond(touches, add_tile, lambda before: before, running_sum)

    density = lax.fori_loop(0, live_count, add_pair, jnp.zeros((BLK,), jnp.float32))
    return (density * valid_rows).reshape(1, BLK)


def general(mesh):
    placed = (P(("wide", "grp"), None), P(("wide", "grp")), P(("wide", "grp")))
    return jax.shard_map(
        per_device, mesh=mesh, in_specs=placed, out_specs=P(("wide", "grp"), None), check_vma=False
    )


MESH = pl.DeviceIdType.MESH
SCALE = SHARPNESS * math.log2(math.e)
NEVER = -1e30
MARK = 4.0


def rows_times_rows(left, right, precision=None):
    return lax.dot_general(
        left, right, (((1,), (1,)), ((), ())), precision=precision,
        preferred_element_type=jnp.float32,
    )


def thirds(values, axis):
    high = values.astype(jnp.bfloat16)
    rest = values - high.astype(jnp.float32)
    middle = rest.astype(jnp.bfloat16)
    low = (rest - middle.astype(jnp.float32)).astype(jnp.bfloat16)
    return jnp.concatenate([high, middle, low], axis=axis)


def gather_kernel(
    n_wide, n_grp, cap, embeds_ref, bucket_ref, pairs_ref, out_ref,
    rows, bucket_row, entries, outgoing, panel, sums, result,
    load_sem, send_sem, pass_sem, recv_sem, give_sem, take_sem,
):
    me_wide, me_grp = lax.axis_index("wide"), lax.axis_index("grp")
    parity = lax.rem(me_wide, 2)
    my_home = n_grp // 2 - parity
    is_home = me_grp == my_home
    row_dev, width = rows.shape
    block = n_wide * cap
    devices = n_wide * n_grp
    half = n_wide // 2

    def order_of(grp, odd):
        along = grp + odd * (n_grp - 1 - 2 * grp)
        return jnp.where(along >= n_grp // 2, along - n_grp // 2, n_grp - 1 - along)

    def grp_of(order, odd):
        along = order + n_grp // 2 if order < n_grp // 2 else n_grp - 1 - order
        return along + odd * (n_grp - 1 - 2 * along)

    load = pltpu.make_async_copy(embeds_ref, rows, load_sem.at[0])
    load.start()
    load_bucket = pltpu.make_async_copy(bucket_ref, bucket_row, load_sem.at[1])
    load_bucket.start()
    load_pairs = pltpu.make_async_copy(pairs_ref, entries, load_sem.at[2])
    load_pairs.start()
    barrier = pltpu.get_barrier_semaphore()

    for step in range(1, n_wide):
        pl.semaphore_signal(
            barrier, inc=1, device_id=(lax.rem(me_wide + step, n_wide), me_grp),
            device_id_type=MESH,
        )

    @pl.when(is_home)
    def _():
        for step in range(1, n_grp):
            pl.semaphore_signal(
                barrier, inc=1, device_id=(me_wide, lax.rem(me_grp + step, n_grp)),
                device_id_type=MESH,
            )

    @pl.when(jnp.logical_not(is_home))
    def _():
        pl.semaphore_signal(
            barrier, inc=1, device_id=(me_wide, my_home), device_id_type=MESH
        )

    load_bucket.wait()
    bucket = bucket_row[...].reshape(1, row_dev)
    of_bucket = lax.broadcasted_iota(jnp.int32, (n_wide, row_dev), 0) == bucket
    onehot = of_bucket.astype(jnp.float32)
    earlier = (
        lax.broadcasted_iota(jnp.int32, (row_dev, row_dev), 0)
        < lax.broadcasted_iota(jnp.int32, (row_dev, row_dev), 1)
    ).astype(jnp.float32).astype(jnp.bfloat16)
    before = jnp.dot(onehot.astype(jnp.bfloat16), earlier, preferred_element_type=jnp.float32)
    rank = jnp.sum(before * onehot, axis=0, keepdims=True).astype(jnp.int32)
    counts = jnp.sum(onehot, axis=1, keepdims=True).astype(jnp.int32)
    slots = (bucket >> 1) * cap + rank

    load.wait()
    floats = rows[...].astype(jnp.float32)
    unit = (
        floats * lax.rsqrt(jnp.sum(floats * floats, axis=1, keepdims=True) + EPSILON)
    ).astype(jnp.bfloat16)
    first_lane = lax.broadcasted_iota(jnp.int32, (cap, 128), 1) == 0
    within = lax.broadcasted_iota(jnp.int32, (cap, 128), 0)

    odd_of = [1 - lax.rem(me_grp, 2), lax.rem(me_grp, 2)]

    def fill(turn):
        odd = odd_of[turn]
        mine = jnp.where((bucket & 1) == odd, slots, -1)
        chosen = (
            lax.broadcasted_iota(jnp.int32, (half * cap, row_dev), 0) == mine
        ).astype(jnp.float32).astype(jnp.bfloat16)
        placed = jnp.dot(chosen, unit, preferred_element_type=jnp.float32)
        for m in range(half):
            piece = placed[m * cap : (m + 1) * cap]
            held = jnp.where(odd == 0, counts[2 * m : 2 * m + 1], counts[2 * m + 1 : 2 * m + 2])
            padding = first_lane & (within >= held)
            at = turn * half + m
            outgoing[at, :, :128] = jnp.where(padding, MARK, piece[:, :128]).astype(jnp.bfloat16)
            outgoing[at, :, 128:] = piece[:, 128:].astype(jnp.bfloat16)

    def piece_copy(turn, step):
        odd = odd_of[turn]
        m = lax.rem(me_wide // 2 + step, half)
        place = order_of(me_grp, odd) * n_wide + 2 * step + parity
        return pltpu.make_async_remote_copy(
            src_ref=outgoing.at[turn * half + m],
            dst_ref=panel.at[pl.ds(pl.multiple_of(place * cap, cap), cap)],
            send_sem=send_sem.at[turn * half + m], recv_sem=recv_sem.at[place],
            device_id=(2 * m + odd, me_grp), device_id_type=MESH,
        )

    fill(0)

    @pl.when(is_home)
    def _():
        pl.semaphore_wait(barrier, n_wide - 1 + n_grp - 1)

    @pl.when(jnp.logical_not(is_home))
    def _():
        pl.semaphore_wait(barrier, n_wide - 1 + 1)

    my_order = order_of(me_grp, parity)

    def panel_slot(place):
        return panel.at[pl.ds(pl.multiple_of(place * cap, cap), cap)]

    def arrive(place):
        pltpu.make_async_copy(panel_slot(place), panel_slot(place), recv_sem.at[place]).wait()

    def pass_on(index):
        place = my_order * n_wide + index
        return pltpu.make_async_remote_copy(
            src_ref=panel_slot(place), dst_ref=panel_slot(place),
            send_sem=pass_sem.at[index], recv_sem=recv_sem.at[place],
            device_id=(me_wide, my_home), device_id_type=MESH,
        )

    def send(turn):
        @pl.when(odd_of[turn] == parity)
        def _():
            place = my_order * n_wide + parity
            pltpu.make_async_copy(
                outgoing.at[turn * half + me_wide // 2], panel_slot(place), recv_sem.at[place]
            ).start()

        @pl.when(odd_of[turn] != parity)
        def _():
            piece_copy(turn, 0).start()

        for step in range(1, half):
            piece_copy(turn, step).start()

    send(0)
    fill(1)
    send(1)
    is_far = my_order == n_grp - 1

    @pl.when(is_far)
    def _():
        for index in range(n_wide):
            arrive(my_order * n_wide + index)
        for index in range(n_wide):
            pass_on(index).start()

    @pl.when(jnp.logical_not(is_far | is_home))
    def _():
        for index in range(n_wide):
            arrive(my_order * n_wide + index)
            pass_on(index).start()

    def shard_order(axis):
        slot = lax.broadcasted_iota(jnp.int32, (block, block), axis)
        mine = me_wide // 2
        step = jnp.zeros((block, block), jnp.int32)
        for t in range(1, half):
            step = step + (slot >= 2 * t * cap).astype(jnp.int32)
        wraps = (step > mine).astype(jnp.int32)
        return slot + cap * (2 * mine - 4 * step + n_wide * wraps)

    sooner = (shard_order(0) < shard_order(1)).astype(jnp.float32).astype(jnp.bfloat16)
    load_pairs.wait()
    weights = []
    for k in range(n_grp):
        named = grp_of(k, parity)
        weight = jnp.float32(0.0)
        for p in range(entries.shape[0]):
            weight = weight + jnp.where(entries[p] == named, 1.0, 0.0)
        weights.append(weight)

    @pl.when(is_home)
    def _():
        pick = (
            (lax.broadcasted_iota(jnp.int32, (8, 128), 1) == 0)
            .astype(jnp.float32).astype(jnp.bfloat16)
        )
        ones = jnp.ones((8, 3 * 128), jnp.bfloat16)

        def lane_flags(first, count):
            return rows_times_rows(pick, panel[first : first + count, :128])[0:1] < 2.0

        def fold(e, lanes):
            folded = e[:, :128]
            for lane in range(128, lanes, 128):
                folded = folded + e[:, lane : lane + 128]
            return folded

        def row_sums(folded):
            return rows_times_rows(ones, thirds(folded, 1))[0:1]

        lane_bias = []
        for k in range(n_grp):
            base = k * block
            step_rows = 128 if k == n_grp - 1 else block
            own_bias = []
            arrived = 0
            for start in range(0, block, step_rows):
                stop = start + step_rows
                while arrived * cap < stop:
                    arrive(k * n_wide + arrived)
                    arrived += 1
                left = panel[base + start : base + stop]
                bias = jnp.where(left[:, 0:1].astype(jnp.float32) < 2.0, -SCALE, NEVER)
                valid = lane_flags(base + start, step_rows)
                sums[k, n_grp : n_grp + 1, start:stop] = valid.astype(jnp.float32)
                own_bias.append(jnp.where(valid, 0.0, NEVER))
                for b in range(k):
                    right = panel[b * block : (b + 1) * block]
                    e = jnp.exp2(rows_times_rows(left, right) * SCALE + bias + lane_bias[b])
                    down = jnp.sum(e, axis=0, keepdims=True)
                    if start == 0:
                        sums[b, k : k + 1, :] = down
                    else:
                        sums[b, k : k + 1, :] += down
                    sums[k, b : b + 1, start:stop] = row_sums(fold(e, block))
                right = panel[base : base + stop]
                e = jnp.exp2(
                    rows_times_rows(left, right) * SCALE + bias
                    + jnp.concatenate(own_bias, axis=1)
                )
                down = jnp.sum(e, axis=0, keepdims=True)
                if start == 0:
                    sums[k, k : k + 1, start:stop] = down
                else:
                    sums[k, k : k + 1, :start] += down[:, :start]
                    sums[k, k : k + 1, start:stop] = down[:, start:] + row_sums(fold(e, start))
            lane_bias.append(jnp.concatenate(own_bias, axis=1))

        keep = pltpu.make_async_copy(sums.at[0], result, take_sem)
        keep.start()
        gives = []
        for k in range(1, n_grp):
            give = pltpu.make_async_remote_copy(
                src_ref=sums.at[k], dst_ref=result,
                send_sem=give_sem.at[k], recv_sem=take_sem,
                device_id=(me_wide, grp_of(k, parity)), device_id_type=MESH,
            )
            give.start()
            gives.append(give)
        for give in gives:
            give.wait_send()

    pltpu.make_async_copy(result, result, take_sem).wait()
    got = result[...]
    flags = got[n_grp : n_grp + 1]
    ahead = jnp.dot(
        jnp.broadcast_to(flags, (8, block)).astype(jnp.bfloat16), sooner,
        preferred_element_type=jnp.float32,
    )[0:1]
    slot_place = jnp.where(flags > 0.5, ahead, -1.0).astype(jnp.int32)
    position = lax.broadcasted_iota(jnp.int32, (block, block), 0)
    squeeze = (position == slot_place).astype(jnp.float32).astype(jnp.bfloat16)
    total = jnp.zeros((1, block), jnp.float32)
    for k in range(n_grp):
        total = total + got[k : k + 1] * weights[k]
    squeezed = rows_times_rows(
        thirds(jnp.broadcast_to(total, (16, block)), 0), squeeze
    )
    out_ref[...] = squeezed[0:1] + squeezed[16:17] + squeezed[32:33]

    for turn in range(2):
        @pl.when(odd_of[turn] != parity)
        def _():
            piece_copy(turn, 0).wait_send()

        for step in range(1, half):
            piece_copy(turn, step).wait_send()

    @pl.when(jnp.logical_not(is_home))
    def _():
        for index in range(n_wide):
            pass_on(index).wait_send()


def gathered(embeds, bucket, pairs):
    n_wide, n_grp = lax.axis_size("wide"), lax.axis_size("grp")
    row_dev, width = embeds.shape
    cap = BLK // n_wide
    return pl.pallas_call(
        functools.partial(gather_kernel, n_wide, n_grp, cap),
        out_shape=jax.ShapeDtypeStruct((1, BLK), jnp.float32),
        in_specs=[pl.BlockSpec(memory_space=pl.ANY)] * 3,
        out_specs=pl.BlockSpec(memory_space=pltpu.VMEM),
        scratch_shapes=[
            pltpu.VMEM((row_dev, width), embeds.dtype),
            pltpu.VMEM((row_dev,), jnp.int32),
            pltpu.SMEM(pairs.shape, jnp.int32),
            pltpu.VMEM((n_wide, cap, width), jnp.bfloat16),
            pltpu.VMEM((n_grp * BLK, width), jnp.bfloat16),
            pltpu.VMEM((n_grp, 8, BLK), jnp.float32),
            pltpu.VMEM((8, BLK), jnp.float32),
            pltpu.SemaphoreType.DMA((3,)),
            pltpu.SemaphoreType.DMA((n_wide,)),
            pltpu.SemaphoreType.DMA((n_wide,)),
            pltpu.SemaphoreType.DMA((n_wide * n_grp,)),
            pltpu.SemaphoreType.DMA((n_grp,)),
            pltpu.SemaphoreType.DMA,
        ],
        compiler_params=pltpu.CompilerParams(
            collective_id=0, has_side_effects=True, vmem_limit_bytes=60 * 1024 * 1024
        ),
        cost_estimate=pl.CostEstimate(
            flops=20 * BLK * BLK * width, bytes_accessed=2 * row_dev * width,
            transcendentals=10 * BLK * BLK,
        ),
    )(embeds, bucket, pairs)


def solution(mesh):
    n_wide, n_grp = mesh.shape["wide"], mesh.shape["grp"]
    if n_grp != 4 or (BLK // n_wide) % 16:
        return general(mesh)
    placed = (P(("wide", "grp"), None), P(("wide", "grp")), P(("wide", "grp")))
    return jax.shard_map(
        gathered, mesh=mesh, in_specs=placed, out_specs=P(("wide", "grp"), None), check_vma=False
    )
```

```python
import jax
import jax.numpy as jnp
from jax import lax
from jax.experimental import pallas as pl
from jax.experimental.pallas import tpu as pltpu
from jax.sharding import PartitionSpec as P
import functools
import math

BLK = 384


SHARPNESS = 10.0
EPSILON = 1e-06


def pair_sums(left_rows, right_rows, right_weight):
    cosines = lax.dot_general(
        left_rows, right_rows, (((1,), (1,)), ((), ())), preferred_element_type=jnp.float32
    )
    return jnp.sum(jnp.exp(SHARPNESS * (cosines - 1.0)) * right_weight[None, :], axis=1)


def per_device(embeds, bucket, pairs):
    wide_count = lax.axis_size("wide")
    feature_width = embeds.shape[1]
    capacity = BLK // wide_count
    floats = embeds.astype(jnp.float32)
    unit_rows = (
        floats * lax.rsqrt(jnp.sum(floats * floats, axis=1, keepdims=True) + EPSILON)
    ).astype(jnp.bfloat16)
    onehot = (bucket[:, None] == jnp.arange(wide_count, dtype=jnp.int32)[None, :]).astype(jnp.int32)
    row_ranks = jnp.sum(jnp.cumsum(onehot, axis=0) * onehot, axis=1) - 1
    counts = jnp.sum(onehot, axis=0)
    send_slots = bucket * capacity + row_ranks
    outgoing = (
        jnp.zeros((wide_count * capacity, feature_width), jnp.bfloat16)
        .at[send_slots]
        .set(unit_rows)
    )
    received, arrived = (
        lax.all_to_all(
            outgoing.reshape(wide_count, capacity, feature_width),
            "wide",
            split_axis=0,
            concat_axis=0,
            tiled=True,
        ),
        lax.all_to_all(
            counts.reshape(wide_count, 1), "wide", split_axis=0, concat_axis=0, tiled=True
        ),
    )
    arrived = arrived.reshape(wide_count)
    offsets = jnp.cumsum(arrived) - arrived
    within = jnp.arange(capacity, dtype=jnp.int32)
    places = jnp.where(within[None, :] < arrived[:, None], offsets[:, None] + within[None, :], BLK)
    own_block = (
        jnp.zeros((BLK, feature_width), jnp.bfloat16)
        .at[places.reshape(-1)]
        .set(received.reshape(wide_count * capacity, feature_width), mode="drop")
    )
    total_rows = jnp.sum(arrived)
    valid_rows = (jnp.arange(BLK, dtype=jnp.int32) < total_rows).astype(jnp.float32)
    flags_wire = valid_rows.astype(jnp.bfloat16)
    live_count = jnp.sum((pairs >= 0).astype(jnp.int32))
    first_row = jnp.int32(0)
    panel_rows = lax.all_gather(own_block, "grp", axis=0, tiled=True)
    panel_flags = lax.all_gather(flags_wire, "grp", axis=0, tiled=True)
    length = panel_rows.shape[0]
    span_rows = min(BLK, length)

    def add_pair(pair_index, running_sum):
        target = pairs[pair_index] * BLK
        shift_rows = jnp.clip(target, 0, length - span_rows)

        def add_tile(before):
            right_rows = lax.dynamic_slice_in_dim(panel_rows, shift_rows, span_rows, 0)
            right_flags = lax.dynamic_slice_in_dim(panel_flags, shift_rows, span_rows, 0).astype(
                jnp.float32
            )
            global_rows = shift_rows + jnp.arange(span_rows, dtype=jnp.int32)
            inside = (global_rows >= target) & (global_rows < target + BLK)
            return before + pair_sums(own_block, right_rows, jnp.where(inside, right_flags, 0.0))

        touches = (target < first_row + length) & (target + BLK > first_row)
        return lax.cond(touches, add_tile, lambda before: before, running_sum)

    density = lax.fori_loop(0, live_count, add_pair, jnp.zeros((BLK,), jnp.float32))
    return (density * valid_rows).reshape(1, BLK)


def general(mesh):
    placed = (P(("wide", "grp"), None), P(("wide", "grp")), P(("wide", "grp")))
    return jax.shard_map(
        per_device, mesh=mesh, in_specs=placed, out_specs=P(("wide", "grp"), None), check_vma=False
    )


MESH = pl.DeviceIdType.MESH
SCALE = SHARPNESS * math.log2(math.e)
NEVER = -1e30
MARK = 4.0


def rows_times_rows(left, right, precision=None):
    return lax.dot_general(
        left, right, (((1,), (1,)), ((), ())), precision=precision,
        preferred_element_type=jnp.float32,
    )


def thirds(values, axis):
    high = values.astype(jnp.bfloat16)
    rest = values - high.astype(jnp.float32)
    middle = rest.astype(jnp.bfloat16)
    low = (rest - middle.astype(jnp.float32)).astype(jnp.bfloat16)
    return jnp.concatenate([high, middle, low], axis=axis)


def gather_kernel(
    n_wide, n_grp, cap, embeds_ref, bucket_ref, pairs_ref, out_ref,
    rows, bucket_row, entries, outgoing, panel, sums, result, own_sum, squeeze,
    load_sem, send_sem, pass_sem, recv_sem, give_sem, take_sem,
):
    me_wide, me_grp = lax.axis_index("wide"), lax.axis_index("grp")
    parity = lax.rem(me_wide, 2)
    my_home = n_grp // 2 - parity
    is_home = me_grp == my_home
    row_dev, width = rows.shape
    block = n_wide * cap
    devices = n_wide * n_grp
    half = n_wide // 2

    def order_of(grp, odd):
        along = grp + odd * (n_grp - 1 - 2 * grp)
        return jnp.where(along >= n_grp // 2, along - n_grp // 2, n_grp - 1 - along)

    def grp_of(order, odd):
        along = order + n_grp // 2 if order < n_grp // 2 else n_grp - 1 - order
        return along + odd * (n_grp - 1 - 2 * along)

    load = pltpu.make_async_copy(embeds_ref, rows, load_sem.at[0])
    load.start()
    load_bucket = pltpu.make_async_copy(bucket_ref, bucket_row, load_sem.at[1])
    load_bucket.start()
    load_pairs = pltpu.make_async_copy(pairs_ref, entries, load_sem.at[2])
    load_pairs.start()
    barrier = pltpu.get_barrier_semaphore()

    for step in range(1, n_wide):
        pl.semaphore_signal(
            barrier, inc=1, device_id=(lax.rem(me_wide + step, n_wide), me_grp),
            device_id_type=MESH,
        )

    @pl.when(is_home)
    def _():
        for step in range(1, n_grp):
            pl.semaphore_signal(
                barrier, inc=1, device_id=(me_wide, lax.rem(me_grp + step, n_grp)),
                device_id_type=MESH,
            )

    @pl.when(jnp.logical_not(is_home))
    def _():
        pl.semaphore_signal(
            barrier, inc=1, device_id=(me_wide, my_home), device_id_type=MESH
        )

    load_bucket.wait()
    bucket = bucket_row[...].reshape(1, row_dev)
    of_bucket = lax.broadcasted_iota(jnp.int32, (n_wide, row_dev), 0) == bucket
    onehot = of_bucket.astype(jnp.float32)
    earlier = (
        lax.broadcasted_iota(jnp.int32, (row_dev, row_dev), 0)
        < lax.broadcasted_iota(jnp.int32, (row_dev, row_dev), 1)
    ).astype(jnp.float32).astype(jnp.bfloat16)
    before = jnp.dot(onehot.astype(jnp.bfloat16), earlier, preferred_element_type=jnp.float32)
    rank = jnp.sum(before * onehot, axis=0, keepdims=True).astype(jnp.int32)
    counts = jnp.sum(onehot, axis=1, keepdims=True).astype(jnp.int32)
    slots = (bucket >> 1) * cap + rank

    load.wait()
    floats = rows[...].astype(jnp.float32)
    unit = (
        floats * lax.rsqrt(jnp.sum(floats * floats, axis=1, keepdims=True) + EPSILON)
    ).astype(jnp.bfloat16)
    first_lane = lax.broadcasted_iota(jnp.int32, (cap, 128), 1) == 0
    within = lax.broadcasted_iota(jnp.int32, (cap, 128), 0)

    odd_of = [1 - lax.rem(me_grp, 2), lax.rem(me_grp, 2)]

    def fill(turn):
        odd = odd_of[turn]
        mine = jnp.where((bucket & 1) == odd, slots, -1)
        chosen = (
            lax.broadcasted_iota(jnp.int32, (half * cap, row_dev), 0) == mine
        ).astype(jnp.float32).astype(jnp.bfloat16)
        placed = jnp.dot(chosen, unit, preferred_element_type=jnp.float32)
        for m in range(half):
            piece = placed[m * cap : (m + 1) * cap]
            held = jnp.where(odd == 0, counts[2 * m : 2 * m + 1], counts[2 * m + 1 : 2 * m + 2])
            padding = first_lane & (within >= held)
            at = turn * half + m
            outgoing[at, :, :128] = jnp.where(padding, MARK, piece[:, :128]).astype(jnp.bfloat16)
            outgoing[at, :, 128:] = piece[:, 128:].astype(jnp.bfloat16)

    def piece_copy(turn, step):
        odd = odd_of[turn]
        m = lax.rem(me_wide // 2 + step, half)
        place = order_of(me_grp, odd) * n_wide + 2 * step + parity
        return pltpu.make_async_remote_copy(
            src_ref=outgoing.at[turn * half + m],
            dst_ref=panel.at[pl.ds(pl.multiple_of(place * cap, cap), cap)],
            send_sem=send_sem.at[turn * half + m], recv_sem=recv_sem.at[place],
            device_id=(2 * m + odd, me_grp), device_id_type=MESH,
        )

    fill(0)

    @pl.when(is_home)
    def _():
        pl.semaphore_wait(barrier, n_wide - 1 + n_grp - 1)

    @pl.when(jnp.logical_not(is_home))
    def _():
        pl.semaphore_wait(barrier, n_wide - 1 + 1)

    my_order = order_of(me_grp, parity)

    def panel_slot(place):
        return panel.at[pl.ds(pl.multiple_of(place * cap, cap), cap)]

    def arrive(place):
        pltpu.make_async_copy(panel_slot(place), panel_slot(place), recv_sem.at[place]).wait()

    def pass_on(index):
        place = my_order * n_wide + index
        return pltpu.make_async_remote_copy(
            src_ref=panel_slot(place), dst_ref=panel_slot(place),
            send_sem=pass_sem.at[index], recv_sem=recv_sem.at[place],
            device_id=(me_wide, my_home), device_id_type=MESH,
        )

    def send(turn):
        @pl.when(odd_of[turn] == parity)
        def _():
            place = my_order * n_wide + parity
            pltpu.make_async_copy(
                outgoing.at[turn * half + me_wide // 2], panel_slot(place), recv_sem.at[place]
            ).start()

        @pl.when(odd_of[turn] != parity)
        def _():
            piece_copy(turn, 0).start()

        for step in range(1, half):
            piece_copy(turn, step).start()

    send(0)
    fill(1)
    send(1)
    is_far = my_order == n_grp - 1

    @pl.when(is_far)
    def _():
        for index in range(half):
            arrive(my_order * n_wide + index)
        for index in range(half):
            pass_on(index).start()
        for index in range(half, n_wide):
            arrive(my_order * n_wide + index)
            pass_on(index).start()

    @pl.when(jnp.logical_not(is_far | is_home))
    def _():
        for index in range(n_wide):
            arrive(my_order * n_wide + index)
            pass_on(index).start()

    def shard_order(axis):
        slot = lax.broadcasted_iota(jnp.int32, (block, block), axis)
        mine = me_wide // 2
        step = jnp.zeros((block, block), jnp.int32)
        for t in range(1, half):
            step = step + (slot >= 2 * t * cap).astype(jnp.int32)
        wraps = (step > mine).astype(jnp.int32)
        return slot + cap * (2 * mine - 4 * step + n_wide * wraps)

    sooner = (shard_order(0) < shard_order(1)).astype(jnp.float32).astype(jnp.bfloat16)
    load_pairs.wait()
    weights = []
    for k in range(n_grp):
        named = grp_of(k, parity)
        weight = jnp.float32(0.0)
        for p in range(entries.shape[0]):
            weight = weight + jnp.where(entries[p] == named, 1.0, 0.0)
        weights.append(weight)
    own_weight = jnp.float32(0.0)
    for p in range(entries.shape[0]):
        own_weight = own_weight + jnp.where(entries[p] == me_grp, 1.0, 0.0)

    pick = (
        (lax.broadcasted_iota(jnp.int32, (8, 128), 1) == 0)
        .astype(jnp.float32).astype(jnp.bfloat16)
    )

    def lane_flags(first, count):
        lead = panel[pl.ds(first, count), :128]
        return rows_times_rows(pick, lead)[0:1] < 2.0

    def own_part():
        first = pl.multiple_of(my_order * block, block)
        own = panel[pl.ds(first, block), :]
        valid = lane_flags(first, block)
        bias = jnp.where(own[:, 0:1].astype(jnp.float32) < 2.0, -SCALE, NEVER)
        e = jnp.exp2(
            rows_times_rows(own, own) * SCALE + bias + jnp.where(valid, 0.0, NEVER)
        )
        own_sum[0:1, :] = jnp.sum(e, axis=0, keepdims=True)
        ahead = jnp.dot(
            jnp.broadcast_to(valid.astype(jnp.float32), (8, block)).astype(jnp.bfloat16),
            sooner, preferred_element_type=jnp.float32,
        )[0:1]
        slot_place = jnp.where(valid, ahead, -1.0).astype(jnp.int32)
        position = lax.broadcasted_iota(jnp.int32, (block, block), 0)
        squeeze[...] = (position == slot_place).astype(jnp.float32).astype(jnp.bfloat16)

    @pl.when(jnp.logical_not(is_home))
    def _():
        own_part()

    @pl.when(is_home)
    def _():
        ones = jnp.ones((8, 3 * 128), jnp.bfloat16)

        def fold(e, lanes):
            folded = e[:, :128]
            for lane in range(128, lanes, 128):
                folded = folded + e[:, lane : lane + 128]
            return folded

        def row_sums(folded):
            return rows_times_rows(ones, thirds(folded, 1))[0:1]

        lane_bias = []
        for k in range(n_grp):
            sums[k, k : k + 1, :] = jnp.zeros((1, block), jnp.float32)
        for k in range(n_grp):
            base = k * block
            step_rows = 128 if k == n_grp - 1 else block
            own_bias = []
            arrived = 0
            for start in range(0, block, step_rows):
                stop = start + step_rows
                while arrived * cap < stop:
                    arrive(k * n_wide + arrived)
                    arrived += 1
                left = panel[base + start : base + stop]
                bias = jnp.where(left[:, 0:1].astype(jnp.float32) < 2.0, -SCALE, NEVER)
                valid = lane_flags(base + start, step_rows)
                own_bias.append(jnp.where(valid, 0.0, NEVER))
                for b in range(k):
                    right = panel[b * block : (b + 1) * block]
                    e = jnp.exp2(rows_times_rows(left, right) * SCALE + bias + lane_bias[b])
                    down = jnp.sum(e, axis=0, keepdims=True)
                    if start == 0:
                        sums[b, k : k + 1, :] = down
                    else:
                        sums[b, k : k + 1, :] += down
                    sums[k, b : b + 1, start:stop] = row_sums(fold(e, block))
            lane_bias.append(jnp.concatenate(own_bias, axis=1))
            if k == 0:
                own_part()

        keep = pltpu.make_async_copy(sums.at[0], result, take_sem)
        keep.start()
        gives = []
        for k in range(1, n_grp):
            give = pltpu.make_async_remote_copy(
                src_ref=sums.at[k], dst_ref=result,
                send_sem=give_sem.at[k], recv_sem=take_sem,
                device_id=(me_wide, grp_of(k, parity)), device_id_type=MESH,
            )
            give.start()
            gives.append(give)
        for give in gives:
            give.wait_send()

    pltpu.make_async_copy(result, result, take_sem).wait()
    got = result[...]
    total = own_sum[0:1, :] * own_weight
    for k in range(n_grp):
        total = total + got[k : k + 1] * weights[k]
    squeezed = rows_times_rows(
        thirds(jnp.broadcast_to(total, (16, block)), 0), squeeze[...]
    )
    out_ref[...] = squeezed[0:1] + squeezed[16:17] + squeezed[32:33]

    for turn in range(2):
        @pl.when(odd_of[turn] != parity)
        def _():
            piece_copy(turn, 0).wait_send()

        for step in range(1, half):
            piece_copy(turn, step).wait_send()

    @pl.when(jnp.logical_not(is_home))
    def _():
        for index in range(n_wide):
            pass_on(index).wait_send()


def gathered(embeds, bucket, pairs):
    n_wide, n_grp = lax.axis_size("wide"), lax.axis_size("grp")
    row_dev, width = embeds.shape
    cap = BLK // n_wide
    return pl.pallas_call(
        functools.partial(gather_kernel, n_wide, n_grp, cap),
        out_shape=jax.ShapeDtypeStruct((1, BLK), jnp.float32),
        in_specs=[pl.BlockSpec(memory_space=pl.ANY)] * 3,
        out_specs=pl.BlockSpec(memory_space=pltpu.VMEM),
        scratch_shapes=[
            pltpu.VMEM((row_dev, width), embeds.dtype),
            pltpu.VMEM((row_dev,), jnp.int32),
            pltpu.SMEM(pairs.shape, jnp.int32),
            pltpu.VMEM((n_wide, cap, width), jnp.bfloat16),
            pltpu.VMEM((n_grp * BLK, width), jnp.bfloat16),
            pltpu.VMEM((n_grp, 8, BLK), jnp.float32),
            pltpu.VMEM((8, BLK), jnp.float32),
            pltpu.VMEM((8, BLK), jnp.float32),
            pltpu.VMEM((BLK, BLK), jnp.bfloat16),
            pltpu.SemaphoreType.DMA((3,)),
            pltpu.SemaphoreType.DMA((n_wide,)),
            pltpu.SemaphoreType.DMA((n_wide,)),
            pltpu.SemaphoreType.DMA((n_wide * n_grp,)),
            pltpu.SemaphoreType.DMA((n_grp,)),
            pltpu.SemaphoreType.DMA,
        ],
        compiler_params=pltpu.CompilerParams(
            collective_id=0, has_side_effects=True, vmem_limit_bytes=60 * 1024 * 1024
        ),
        cost_estimate=pl.CostEstimate(
            flops=20 * BLK * BLK * width, bytes_accessed=2 * row_dev * width,
            transcendentals=10 * BLK * BLK,
        ),
    )(embeds, bucket, pairs)


def solution(mesh):
    n_wide, n_grp = mesh.shape["wide"], mesh.shape["grp"]
    if n_grp != 4 or (BLK // n_wide) % 16:
        return general(mesh)
    placed = (P(("wide", "grp"), None), P(("wide", "grp")), P(("wide", "grp")))
    return jax.shard_map(
        gathered, mesh=mesh, in_specs=placed, out_specs=P(("wide", "grp"), None), check_vma=False
    )
```

```python
import jax
import jax.numpy as jnp
from jax import lax
from jax.experimental import pallas as pl
from jax.experimental.pallas import tpu as pltpu
from jax.sharding import PartitionSpec as P
import functools
import math

BLK = 384


SHARPNESS = 10.0
EPSILON = 1e-06


def pair_sums(left_rows, right_rows, right_weight):
    cosines = lax.dot_general(
        left_rows, right_rows, (((1,), (1,)), ((), ())), preferred_element_type=jnp.float32
    )
    return jnp.sum(jnp.exp(SHARPNESS * (cosines - 1.0)) * right_weight[None, :], axis=1)


def per_device(embeds, bucket, pairs):
    wide_count = lax.axis_size("wide")
    feature_width = embeds.shape[1]
    capacity = BLK // wide_count
    floats = embeds.astype(jnp.float32)
    unit_rows = (
        floats * lax.rsqrt(jnp.sum(floats * floats, axis=1, keepdims=True) + EPSILON)
    ).astype(jnp.bfloat16)
    onehot = (bucket[:, None] == jnp.arange(wide_count, dtype=jnp.int32)[None, :]).astype(jnp.int32)
    row_ranks = jnp.sum(jnp.cumsum(onehot, axis=0) * onehot, axis=1) - 1
    counts = jnp.sum(onehot, axis=0)
    send_slots = bucket * capacity + row_ranks
    outgoing = (
        jnp.zeros((wide_count * capacity, feature_width), jnp.bfloat16)
        .at[send_slots]
        .set(unit_rows)
    )
    received, arrived = (
        lax.all_to_all(
            outgoing.reshape(wide_count, capacity, feature_width),
            "wide",
            split_axis=0,
            concat_axis=0,
            tiled=True,
        ),
        lax.all_to_all(
            counts.reshape(wide_count, 1), "wide", split_axis=0, concat_axis=0, tiled=True
        ),
    )
    arrived = arrived.reshape(wide_count)
    offsets = jnp.cumsum(arrived) - arrived
    within = jnp.arange(capacity, dtype=jnp.int32)
    places = jnp.where(within[None, :] < arrived[:, None], offsets[:, None] + within[None, :], BLK)
    own_block = (
        jnp.zeros((BLK, feature_width), jnp.bfloat16)
        .at[places.reshape(-1)]
        .set(received.reshape(wide_count * capacity, feature_width), mode="drop")
    )
    total_rows = jnp.sum(arrived)
    valid_rows = (jnp.arange(BLK, dtype=jnp.int32) < total_rows).astype(jnp.float32)
    flags_wire = valid_rows.astype(jnp.bfloat16)
    live_count = jnp.sum((pairs >= 0).astype(jnp.int32))
    first_row = jnp.int32(0)
    panel_rows = lax.all_gather(own_block, "grp", axis=0, tiled=True)
    panel_flags = lax.all_gather(flags_wire, "grp", axis=0, tiled=True)
    length = panel_rows.shape[0]
    span_rows = min(BLK, length)

    def add_pair(pair_index, running_sum):
        target = pairs[pair_index] * BLK
        shift_rows = jnp.clip(target, 0, length - span_rows)

        def add_tile(before):
            right_rows = lax.dynamic_slice_in_dim(panel_rows, shift_rows, span_rows, 0)
            right_flags = lax.dynamic_slice_in_dim(panel_flags, shift_rows, span_rows, 0).astype(
                jnp.float32
            )
            global_rows = shift_rows + jnp.arange(span_rows, dtype=jnp.int32)
            inside = (global_rows >= target) & (global_rows < target + BLK)
            return before + pair_sums(own_block, right_rows, jnp.where(inside, right_flags, 0.0))

        touches = (target < first_row + length) & (target + BLK > first_row)
        return lax.cond(touches, add_tile, lambda before: before, running_sum)

    density = lax.fori_loop(0, live_count, add_pair, jnp.zeros((BLK,), jnp.float32))
    return (density * valid_rows).reshape(1, BLK)


def general(mesh):
    placed = (P(("wide", "grp"), None), P(("wide", "grp")), P(("wide", "grp")))
    return jax.shard_map(
        per_device, mesh=mesh, in_specs=placed, out_specs=P(("wide", "grp"), None), check_vma=False
    )


MESH = pl.DeviceIdType.MESH
SCALE = SHARPNESS * math.log2(math.e)
NEVER = -1e30
MARK = 4.0


def rows_times_rows(left, right, precision=None):
    return lax.dot_general(
        left, right, (((1,), (1,)), ((), ())), precision=precision,
        preferred_element_type=jnp.float32,
    )


def thirds(values, axis):
    high = values.astype(jnp.bfloat16)
    rest = values - high.astype(jnp.float32)
    middle = rest.astype(jnp.bfloat16)
    low = (rest - middle.astype(jnp.float32)).astype(jnp.bfloat16)
    return jnp.concatenate([high, middle, low], axis=axis)


def gather_kernel(
    n_wide, n_grp, cap, embeds_ref, bucket_ref, pairs_ref, out_ref,
    rows, bucket_row, entries, outgoing, panel, sums, result, own_sum, squeeze,
    load_sem, send_sem, pass_sem, recv_sem, give_sem, take_sem,
):
    me_wide, me_grp = lax.axis_index("wide"), lax.axis_index("grp")
    parity = lax.rem(me_wide, 2)
    my_home = n_grp // 2 - parity
    is_home = me_grp == my_home
    row_dev, width = rows.shape
    block = n_wide * cap
    devices = n_wide * n_grp
    half = n_wide // 2

    def order_of(grp, odd):
        along = grp + odd * (n_grp - 1 - 2 * grp)
        return jnp.where(along >= n_grp // 2, along - n_grp // 2, n_grp - 1 - along)

    def grp_of(order, odd):
        along = order + n_grp // 2 if order < n_grp // 2 else n_grp - 1 - order
        return along + odd * (n_grp - 1 - 2 * along)

    load = pltpu.make_async_copy(embeds_ref, rows, load_sem.at[0])
    load.start()
    load_bucket = pltpu.make_async_copy(bucket_ref, bucket_row, load_sem.at[1])
    load_bucket.start()
    load_pairs = pltpu.make_async_copy(pairs_ref, entries, load_sem.at[2])
    load_pairs.start()
    barrier = pltpu.get_barrier_semaphore()

    for step in range(1, n_wide):
        pl.semaphore_signal(
            barrier, inc=1, device_id=(lax.rem(me_wide + step, n_wide), me_grp),
            device_id_type=MESH,
        )

    @pl.when(is_home)
    def _():
        for step in range(1, n_grp):
            pl.semaphore_signal(
                barrier, inc=1, device_id=(me_wide, lax.rem(me_grp + step, n_grp)),
                device_id_type=MESH,
            )

    @pl.when(jnp.logical_not(is_home))
    def _():
        pl.semaphore_signal(
            barrier, inc=1, device_id=(me_wide, my_home), device_id_type=MESH
        )

    load_bucket.wait()
    bucket = bucket_row[...].reshape(1, row_dev)
    of_bucket = lax.broadcasted_iota(jnp.int32, (n_wide, row_dev), 0) == bucket
    onehot = of_bucket.astype(jnp.float32)
    earlier = (
        lax.broadcasted_iota(jnp.int32, (row_dev, row_dev), 0)
        < lax.broadcasted_iota(jnp.int32, (row_dev, row_dev), 1)
    ).astype(jnp.float32).astype(jnp.bfloat16)
    before = jnp.dot(onehot.astype(jnp.bfloat16), earlier, preferred_element_type=jnp.float32)
    rank = jnp.sum(before * onehot, axis=0, keepdims=True).astype(jnp.int32)
    counts = jnp.sum(onehot, axis=1, keepdims=True).astype(jnp.int32)
    slots = (bucket >> 1) * cap + rank

    load.wait()
    floats = rows[...].astype(jnp.float32)
    unit = (
        floats * lax.rsqrt(jnp.sum(floats * floats, axis=1, keepdims=True) + EPSILON)
    ).astype(jnp.bfloat16)
    first_lane = lax.broadcasted_iota(jnp.int32, (cap, 128), 1) == 0
    within = lax.broadcasted_iota(jnp.int32, (cap, 128), 0)

    odd_of = [1 - lax.rem(me_grp, 2), lax.rem(me_grp, 2)]

    def fill(turn):
        odd = odd_of[turn]
        mine = jnp.where((bucket & 1) == odd, slots, -1)
        chosen = (
            lax.broadcasted_iota(jnp.int32, (half * cap, row_dev), 0) == mine
        ).astype(jnp.float32).astype(jnp.bfloat16)
        placed = jnp.dot(chosen, unit, preferred_element_type=jnp.float32)
        for m in range(half):
            piece = placed[m * cap : (m + 1) * cap]
            held = jnp.where(odd == 0, counts[2 * m : 2 * m + 1], counts[2 * m + 1 : 2 * m + 2])
            padding = first_lane & (within >= held)
            at = turn * half + m
            outgoing[at, :, :128] = jnp.where(padding, MARK, piece[:, :128]).astype(jnp.bfloat16)
            outgoing[at, :, 128:] = piece[:, 128:].astype(jnp.bfloat16)

    def piece_copy(turn, step):
        odd = odd_of[turn]
        m = lax.rem(me_wide // 2 + step, half)
        place = order_of(me_grp, odd) * n_wide + 2 * step + parity
        return pltpu.make_async_remote_copy(
            src_ref=outgoing.at[turn * half + m],
            dst_ref=panel.at[pl.ds(pl.multiple_of(place * cap, cap), cap)],
            send_sem=send_sem.at[turn * half + m], recv_sem=recv_sem.at[place],
            device_id=(2 * m + odd, me_grp), device_id_type=MESH,
        )

    fill(0)

    @pl.when(is_home)
    def _():
        pl.semaphore_wait(barrier, n_wide - 1 + n_grp - 1)

    @pl.when(jnp.logical_not(is_home))
    def _():
        pl.semaphore_wait(barrier, n_wide - 1 + 1)

    my_order = order_of(me_grp, parity)

    def panel_slot(place):
        return panel.at[pl.ds(pl.multiple_of(place * cap, cap), cap)]

    def arrive(place):
        pltpu.make_async_copy(panel_slot(place), panel_slot(place), recv_sem.at[place]).wait()

    def pass_on(index):
        place = my_order * n_wide + index
        return pltpu.make_async_remote_copy(
            src_ref=panel_slot(place), dst_ref=panel_slot(place),
            send_sem=pass_sem.at[index], recv_sem=recv_sem.at[place],
            device_id=(me_wide, my_home), device_id_type=MESH,
        )

    def send(turn):
        @pl.when(odd_of[turn] == parity)
        def _():
            place = my_order * n_wide + parity
            pltpu.make_async_copy(
                outgoing.at[turn * half + me_wide // 2], panel_slot(place), recv_sem.at[place]
            ).start()

        @pl.when(odd_of[turn] != parity)
        def _():
            piece_copy(turn, 0).start()

        for step in range(1, half):
            piece_copy(turn, step).start()

    send(0)
    fill(1)
    send(1)
    @pl.when(jnp.logical_not(is_home))
    def _():
        for index in range(n_wide):
            arrive(my_order * n_wide + index)
            pass_on(index).start()

    def shard_order(axis):
        slot = lax.broadcasted_iota(jnp.int32, (block, block), axis)
        mine = me_wide // 2
        step = jnp.zeros((block, block), jnp.int32)
        for t in range(1, half):
            step = step + (slot >= 2 * t * cap).astype(jnp.int32)
        wraps = (step > mine).astype(jnp.int32)
        return slot + cap * (2 * mine - 4 * step + n_wide * wraps)

    sooner = (shard_order(0) < shard_order(1)).astype(jnp.float32).astype(jnp.bfloat16)
    load_pairs.wait()
    weights = []
    for k in range(n_grp):
        named = grp_of(k, parity)
        weight = jnp.float32(0.0)
        for p in range(entries.shape[0]):
            weight = weight + jnp.where(entries[p] == named, 1.0, 0.0)
        weights.append(weight)
    own_weight = jnp.float32(0.0)
    for p in range(entries.shape[0]):
        own_weight = own_weight + jnp.where(entries[p] == me_grp, 1.0, 0.0)

    pick = (
        (lax.broadcasted_iota(jnp.int32, (8, 128), 1) == 0)
        .astype(jnp.float32).astype(jnp.bfloat16)
    )

    def lane_flags(first, count):
        lead = panel[pl.ds(first, count), :128]
        return rows_times_rows(pick, lead)[0:1] < 2.0

    def own_part():
        first = pl.multiple_of(my_order * block, block)
        own = panel[pl.ds(first, block), :]
        valid = lane_flags(first, block)
        bias = jnp.where(own[:, 0:1].astype(jnp.float32) < 2.0, -SCALE, NEVER)
        e = jnp.exp2(
            rows_times_rows(own, own) * SCALE + bias + jnp.where(valid, 0.0, NEVER)
        )
        own_sum[0:1, :] = jnp.sum(e, axis=0, keepdims=True)
        ahead = jnp.dot(
            jnp.broadcast_to(valid.astype(jnp.float32), (8, block)).astype(jnp.bfloat16),
            sooner, preferred_element_type=jnp.float32,
        )[0:1]
        slot_place = jnp.where(valid, ahead, -1.0).astype(jnp.int32)
        position = lax.broadcasted_iota(jnp.int32, (block, block), 0)
        squeeze[...] = (position == slot_place).astype(jnp.float32).astype(jnp.bfloat16)

    @pl.when(jnp.logical_not(is_home))
    def _():
        own_part()

    @pl.when(is_home)
    def _():
        ones = jnp.ones((8, 3 * 128), jnp.bfloat16)

        def fold(e, lanes):
            folded = e[:, :128]
            for lane in range(128, lanes, 128):
                folded = folded + e[:, lane : lane + 128]
            return folded

        def row_sums(folded):
            return rows_times_rows(ones, thirds(folded, 1))[0:1]

        def give_copy(k):
            return pltpu.make_async_remote_copy(
                src_ref=sums.at[k], dst_ref=result,
                send_sem=give_sem.at[k], recv_sem=take_sem,
                device_id=(me_wide, grp_of(k, parity)), device_id_type=MESH,
            )

        def give(k):
            if k == 0:
                pltpu.make_async_copy(sums.at[0], result, take_sem).start()
            else:
                give_copy(k).start()

        lane_bias = []
        for k in range(n_grp):
            sums[k, k : k + 1, :] = jnp.zeros((1, block), jnp.float32)
        for k in range(n_grp):
            base = k * block
            step_rows = 128 if k == n_grp - 1 else block
            own_bias = []
            arrived = 0
            for start in range(0, block, step_rows):
                stop = start + step_rows
                while arrived * cap < stop:
                    arrive(k * n_wide + arrived)
                    arrived += 1
                left = panel[base + start : base + stop]
                bias = jnp.where(left[:, 0:1].astype(jnp.float32) < 2.0, -SCALE, NEVER)
                valid = lane_flags(base + start, step_rows)
                own_bias.append(jnp.where(valid, 0.0, NEVER))
                for b in range(k):
                    right = panel[b * block : (b + 1) * block]
                    e = jnp.exp2(rows_times_rows(left, right) * SCALE + bias + lane_bias[b])
                    down = jnp.sum(e, axis=0, keepdims=True)
                    if start == 0:
                        sums[b, k : k + 1, :] = down
                    else:
                        sums[b, k : k + 1, :] += down
                    sums[k, b : b + 1, start:stop] = row_sums(fold(e, block))
                    if k == n_grp - 1 and stop == block:
                        give(b)
            lane_bias.append(jnp.concatenate(own_bias, axis=1))
            if k == 0:
                own_part()

        give(n_grp - 1)
        for k in range(1, n_grp):
            give_copy(k).wait_send()

    pltpu.make_async_copy(result, result, take_sem).wait()
    got = result[...]
    total = own_sum[0:1, :] * own_weight
    for k in range(n_grp):
        total = total + got[k : k + 1] * weights[k]
    squeezed = rows_times_rows(
        thirds(jnp.broadcast_to(total, (16, block)), 0), squeeze[...]
    )
    out_ref[...] = squeezed[0:1] + squeezed[16:17] + squeezed[32:33]

    for turn in range(2):
        @pl.when(odd_of[turn] != parity)
        def _():
            piece_copy(turn, 0).wait_send()

        for step in range(1, half):
            piece_copy(turn, step).wait_send()

    @pl.when(jnp.logical_not(is_home))
    def _():
        for index in range(n_wide):
            pass_on(index).wait_send()


def gathered(embeds, bucket, pairs):
    n_wide, n_grp = lax.axis_size("wide"), lax.axis_size("grp")
    row_dev, width = embeds.shape
    cap = BLK // n_wide
    return pl.pallas_call(
        functools.partial(gather_kernel, n_wide, n_grp, cap),
        out_shape=jax.ShapeDtypeStruct((1, BLK), jnp.float32),
        in_specs=[pl.BlockSpec(memory_space=pl.ANY)] * 3,
        out_specs=pl.BlockSpec(memory_space=pltpu.VMEM),
        scratch_shapes=[
            pltpu.VMEM((row_dev, width), embeds.dtype),
            pltpu.VMEM((row_dev,), jnp.int32),
            pltpu.SMEM(pairs.shape, jnp.int32),
            pltpu.VMEM((n_wide, cap, width), jnp.bfloat16),
            pltpu.VMEM((n_grp * BLK, width), jnp.bfloat16),
            pltpu.VMEM((n_grp, 8, BLK), jnp.float32),
            pltpu.VMEM((8, BLK), jnp.float32),
            pltpu.VMEM((8, BLK), jnp.float32),
            pltpu.VMEM((BLK, BLK), jnp.bfloat16),
            pltpu.SemaphoreType.DMA((3,)),
            pltpu.SemaphoreType.DMA((n_wide,)),
            pltpu.SemaphoreType.DMA((n_wide,)),
            pltpu.SemaphoreType.DMA((n_wide * n_grp,)),
            pltpu.SemaphoreType.DMA((n_grp,)),
            pltpu.SemaphoreType.DMA,
        ],
        compiler_params=pltpu.CompilerParams(
            collective_id=0, has_side_effects=True, vmem_limit_bytes=60 * 1024 * 1024
        ),
        cost_estimate=pl.CostEstimate(
            flops=20 * BLK * BLK * width, bytes_accessed=2 * row_dev * width,
            transcendentals=10 * BLK * BLK,
        ),
    )(embeds, bucket, pairs)


def solution(mesh):
    n_wide, n_grp = mesh.shape["wide"], mesh.shape["grp"]
    if n_grp != 4 or (BLK // n_wide) % 16:
        return general(mesh)
    placed = (P(("wide", "grp"), None), P(("wide", "grp")), P(("wide", "grp")))
    return jax.shard_map(
        gathered, mesh=mesh, in_specs=placed, out_specs=P(("wide", "grp"), None), check_vma=False
    )
```
